32 devices in a mesh: dp: 16 (over z, x, core), tensor: 2 (over y).
Axes of the slice: x: 2, y: 2, z: 4, core: 2. Of those that a mesh axis runs over, the one named last changes fastest.
Arguments:
- o_inputs: bfloat16 [4096, 8192], P('dp', 'tensor'), may hold values from -6 to 6
- o_gradients: bfloat16 [4096, 8192], P('dp', 'tensor'), may hold values from -6 to 6
- up_inputs: bfloat16 [4096, 8192], P('dp', 'tensor'), may hold values from -6 to 6
- up_gradients: bfloat16 [4096, 28672], P('dp', 'tensor'), may hold values from -6 to 6
- o_in_proj: bfloat16 [8192, 32], P('tensor'), may hold values from -0.0625 to 0.0625
- o_out_proj: bfloat16 [8192, 32], P('tensor'), may hold values from -0.0625 to 0.0625
- up_in_proj: bfloat16 [8192, 32], P('tensor'), may hold values from -0.0625 to 0.0625
- up_out_proj: bfloat16 [28672, 32], P('tensor'), may hold values from -0.03125 to 0.03125
- segment_ids: int32 [16, 256], P('dp'), may hold values from 0 to 3, never falling along the last dimension, each value on 1 to 128 neighbouring positions
- owner_map: int32 [16], replicated, may hold values from 0 to 15, each once
Outputs:
- example_vectors: float32 [2, 64, 1024], P(None, 'dp', 'tensor')
- fisher_owned: float32 [16, 128, 1024], P('dp', None, 'tensor')
The draws below stay inside these ranges and needn't reach their ends.
Inputs may be any that keep to these rules, and one draw needn't show every extreme that they name: `segment_ids`: within each row, ids never fall; each of the 4 ids holds 1 to 128 tokens, and one holds exactly that many. `owner_map`: each block index appears exactly once.
All inputs are finite; a program needn't handle non-finite values.
Results may differ from the reference program's by a relative error of at most 0.0003.
Values sent between devices are 32-bit elements; how exact they have to be, the bound alone decides.
No kernel may reach another device: no remote copies, remote signals or barrier semaphores. Data moves between devices by JAX's collectives and lax.ppermute only.
A program may use at most 64 MiB of HBM per device.

```python
import math
import jax
import jax.numpy as jnp
import numpy as np
from jax import lax

D = 8192
FF = 28672
KIN = 32
KOUT = 32
KK = 1024
TOK_DEV = 256
EX_DEV = 4
BLOCKS = 16
TOKENS = 4096
EXAMPLES = 64
OWN_ROWS = 128
N_DP = 16


def level_of(stream_key, dims, cuts, low, top_value):
    loudness, own = 1.0, jax.random.fold_in(stream_key, 6)
    for axis_at, parts in cuts:
        steps = jnp.exp(jax.random.uniform(jax.random.fold_in(own, axis_at), (parts,), jnp.float32, low / len(cuts), top_value / len(cuts)))
        loudness = loudness * jnp.repeat(steps, dims[axis_at] // parts).reshape([-1 if axis == axis_at else 1 for axis in range(len(dims))])
    return loudness


def length_profile(number_of, total, reach, lean):
    loads = [(1 << 20) // math.isqrt(grade ** lean) + 1 for grade in range(2, number_of + 1)]
    surplus, holding = total - reach - (number_of - 1), [1] * (number_of - 1)
    while surplus > 0:
        free = [i for i in range(number_of - 1) if holding[i] < reach]
        whole, budget = sum([loads[i] for i in free]), surplus
        for i in free:
            extra = min(reach - holding[i], max(1, budget * loads[i] // whole), surplus)
            holding[i] = holding[i] + extra
            surplus = surplus - extra
    return np.array([reach] + holding)


def uneven(rng, count, total, limit, lean):
    if count == 2:
        one = jax.random.randint(rng, (), max(1, total - limit), min(limit, total - 1) + 1)
        return jnp.stack([one, total - one])
    lengths = jnp.asarray(length_profile(count, total, limit, lean), jnp.int32)
    pairs = (count - 1) // 2
    donor, sink = lengths[1:1 + 2 * pairs:2], lengths[2:2 + 2 * pairs:2]
    room = jnp.minimum(donor - 1, limit - sink)
    passed = jax.random.randint(jax.random.fold_in(rng, 1), (pairs,), 0, 1 << 20) % (room + 1)
    lengths = lengths.at[1:1 + 2 * pairs:2].set(donor - passed).at[2:2 + 2 * pairs:2].set(sink + passed)
    return lengths[jax.random.permutation(jax.random.fold_in(rng, 2), count)]


def bell_draw(own_key, shape, scale, most, split=(), kind=jnp.bfloat16):
    drawn = scale * jax.random.normal(own_key, shape, jnp.float32)
    if split:
        drawn = drawn * level_of(own_key, shape, split, -0.22, 0.18)
    return jnp.clip(drawn, -most, most).astype(kind)


def setup_inputs(seed: int = 0) -> dict:
    key_list = jax.random.split(jax.random.key(seed), 11)
    o_inputs = bell_draw(key_list[0], (TOKENS, D), 1.0, 6.0, ((0, 16), (1, 2)))
    o_gradients = bell_draw(key_list[1], (TOKENS, D), 1.0, 6.0, ((0, 16), (1, 2)))
    up_inputs = bell_draw(key_list[2], (TOKENS, D), 1.0, 6.0, ((0, 16), (1, 2)))
    up_gradients = bell_draw(key_list[3], (TOKENS, FF), 1.0, 6.0, ((0, 16), (1, 2)))
    o_in_proj = bell_draw(key_list[4], (D, KIN), D ** -0.5, 0.0625, ((0, 2),))
    o_out_proj = bell_draw(key_list[5], (D, KOUT), D ** -0.5, 0.0625, ((0, 2),))
    up_in_proj = bell_draw(key_list[6], (D, KIN), D ** -0.5, 0.0625, ((0, 2),))
    up_out_proj = bell_draw(key_list[7], (FF, KOUT), FF ** -0.5, 0.03125, ((0, 2),))
    segment_ids = jax.vmap(lambda own: jnp.searchsorted(jnp.cumsum(uneven(own, EX_DEV, TOK_DEV, TOK_DEV // 2, 2)), jnp.arange(TOK_DEV), side="right"))(jax.random.split(key_list[8], BLOCKS)).reshape((BLOCKS, TOK_DEV)).astype(jnp.int32)
    owner_map = jax.random.permutation(key_list[9], BLOCKS).astype(jnp.int32)
    return dict(o_inputs=o_inputs, o_gradients=o_gradients, up_inputs=up_inputs, up_gradients=up_gradients, o_in_proj=o_in_proj, o_out_proj=o_out_proj, up_in_proj=up_in_proj, up_out_proj=up_out_proj, segment_ids=segment_ids, owner_map=owner_map)


def vectors(inputs, gradients, in_proj, out_proj, segment_ids):
    in_low = jnp.dot(inputs, in_proj, preferred_element_type=jnp.float32)
    out_low = jnp.dot(gradients, out_proj, preferred_element_type=jnp.float32)
    outers = (out_low[:, :, None] * in_low[:, None, :]).reshape(N_DP, TOK_DEV, KK)
    onehot = (segment_ids[:, :, None] == jnp.arange(EX_DEV, dtype=jnp.int32)[None, None, :]).astype(jnp.float32)
    summed = jnp.einsum("gte,gtk->gek", onehot, outers, precision=lax.Precision.HIGHEST)
    vector_scale = (EX_DEV / TOK_DEV) ** 0.5
    return (summed * vector_scale).reshape(EXAMPLES, KK)


def reference(o_inputs, o_gradients, up_inputs, up_gradients, o_in_proj, o_out_proj, up_in_proj, up_out_proj, segment_ids, owner_map):
    vector_o = vectors(o_inputs, o_gradients, o_in_proj, o_out_proj, segment_ids)
    vector_up = vectors(up_inputs, up_gradients, up_in_proj, up_out_proj, segment_ids)
    example_vectors = jnp.stack([vector_o, vector_up])
    fisher_o = jnp.dot(vector_o.T, vector_o, precision=lax.Precision.HIGHEST) / EXAMPLES
    fisher_up = jnp.dot(vector_up.T, vector_up, precision=lax.Precision.HIGHEST) / EXAMPLES
    stacked = jnp.concatenate([fisher_o, fisher_up], axis=0)
    fisher_owned = stacked.reshape(N_DP, OWN_ROWS, KK)[owner_map]
    return example_vectors, fisher_owned
```

```python
import functools

import jax
import jax.numpy as jnp
from jax import lax
from jax.experimental import pallas as pl
from jax.experimental.pallas import tpu as pltpu
from jax.sharding import PartitionSpec as P

TOK_DEV = 256
EX_DEV = 4
LANES = 128
NT = (((1,), (1,)), ((), ()))
TN = (((0,), (0,)), ((), ()))
VMEM_BYTES = 60 * 2**20
HIGHEST = lax.Precision.HIGHEST


def chunk_plan(widths):
    plan = []
    for which, width in enumerate(widths):
        pieces = max(1, round(width / 4096))
        while width % pieces or (width // pieces) % LANES:
            pieces += 1
        size = width // pieces
        plan += [(which, start, size) for start in range(0, width, size)]
    return plan


def project_kernel(plan, halves, *refs):
    x_hbm, w_hbm, out_ref = refs[0:4], refs[4:8], refs[8]
    x_vmem, w_vmem, x_sem, w_sem = refs[9:13], refs[13:17], refs[17], refs[18]
    w_copies = [pltpu.make_async_copy(w_hbm[i], w_vmem[i], w_sem.at[i]) for i in range(4)]
    x_copies = [
        pltpu.make_async_copy(
            x_hbm[i].at[:, pl.ds(start, size)], x_vmem[i].at[:, pl.ds(start, size)], x_sem.at[n]
        )
        for n, (i, start, size) in enumerate(plan)
    ]
    for n, (i, start, size) in enumerate(plan):
        if start == 0:
            w_copies[i].start()
        x_copies[n].start()
    tokens, rank = x_vmem[0].shape[0], w_vmem[0].shape[0]
    part = tokens // halves
    totals = None
    for n, (i, start, size) in enumerate(plan):
        if start == 0:
            w_copies[i].wait()
        x_copies[n].wait()
        w = w_vmem[i][:, pl.ds(start, size)]
        products = [
            lax.dot_general(
                w, x_vmem[i][pl.ds(h * part, part), pl.ds(start, size)], NT, preferred_element_type=jnp.float32
            )
            for h in range(halves)
        ]
        totals = products if start == 0 else [a + b for a, b in zip(totals, products)]
        if start + size == x_vmem[i].shape[1]:
            for h in range(halves):
                out_ref[pl.ds(i * rank, rank), pl.ds(h * part, part)] = totals[h]


def project(xs, ws):
    plan = chunk_plan([x.shape[1] for x in xs])
    tokens, rank = xs[0].shape[0], ws[0].shape[0]
    return pl.pallas_call(
        functools.partial(project_kernel, plan, 2),
        out_shape=jax.ShapeDtypeStruct((4 * rank, tokens), jnp.float32),
        in_specs=[pl.BlockSpec(memory_space=pl.ANY)] * 8,
        out_specs=pl.BlockSpec(memory_space=pltpu.VMEM),
        scratch_shapes=[pltpu.VMEM(x.shape, x.dtype) for x in xs]
        + [pltpu.VMEM(w.shape, w.dtype) for w in ws]
        + [pltpu.SemaphoreType.DMA((len(plan),)), pltpu.SemaphoreType.DMA((4,))],
        compiler_params=pltpu.CompilerParams(vmem_limit_bytes=VMEM_BYTES),
        name="project",
    )(*xs, *ws)


def vectors_kernel(n_parts, own_rows, *refs):
    parts, seg_ref, owner_ref, vec_ref, send_ref, slabs = refs[:n_parts], *refs[n_parts:]
    low = parts[0][...]
    for other in parts[1:]:
        low = low + other[...]
    rank, tokens = low.shape[0] // 4, low.shape[1]
    fold = LANES // rank
    n_slabs = rank // fold
    col_slabs = vec_ref.shape[2] // LANES
    seg = seg_ref[...]
    rows = EX_DEV * rank
    row = lax.broadcasted_iota(jnp.int32, (rows, LANES), 0)
    lane = lax.broadcasted_iota(jnp.int32, (rows, LANES), 1)
    scale = (EX_DEV / TOK_DEV) ** 0.5
    keep = jnp.where(row % fold == lane // rank, scale, 0.0).astype(jnp.float32)
    to = lax.broadcasted_iota(jnp.int32, (n_slabs * EX_DEV, rows), 0)
    frm = lax.broadcasted_iota(jnp.int32, (n_slabs * EX_DEV, rows), 1)
    gather = (frm // rank == to % EX_DEV) & ((frm % rank) // fold == to // EX_DEV)
    gather = jnp.where(gather, 1.0, 0.0).astype(jnp.float32)
    for p in range(2):
        in_low = low[2 * p * rank : (2 * p + 1) * rank]
        out_low = low[(2 * p + 1) * rank : (2 * p + 2) * rank]
        in_wide = jnp.concatenate([in_low] * fold, axis=0)
        masked = jnp.concatenate([jnp.where(seg == e, out_low, 0.0) for e in range(EX_DEV)], axis=0)
        outer = lax.dot_general(masked, in_wide, NT, precision=HIGHEST, preferred_element_type=jnp.float32)
        flat = jnp.dot(gather, outer * keep, precision=HIGHEST, preferred_element_type=jnp.float32)
        for g in range(n_slabs):
            slabs[p * n_slabs + g] = flat[g * EX_DEV : (g + 1) * EX_DEV]
    t = lax.axis_index("tensor")
    for p in range(2):
        for k in range(col_slabs):
            vec_ref[p, :, pl.ds(k * LANES, LANES)] = slabs[p * n_slabs + t * col_slabs + k]
    for j in range(send_ref.shape[0]):
        first_row = owner_ref[j] * own_rows
        p = first_row // (rank * rank)
        send_ref[j, 0] = slabs[first_row // LANES]
        for k in range(col_slabs):
            send_ref[j, 1 + k] = slabs[p * n_slabs + t * col_slabs + k]


def vectors(parts, segments, owner_map, col_width, own_rows, dp_count):
    n_slabs = (parts[0].shape[0] // 4) ** 2 // LANES
    vmem, smem = pl.BlockSpec(memory_space=pltpu.VMEM), pl.BlockSpec(memory_space=pltpu.SMEM)
    return pl.pallas_call(
        functools.partial(vectors_kernel, len(parts), own_rows),
        out_shape=(
            jax.ShapeDtypeStruct((2, EX_DEV, col_width), jnp.float32),
            jax.ShapeDtypeStruct((dp_count, 1 + col_width // LANES, EX_DEV, LANES), jnp.float32),
        ),
        in_specs=[vmem] * len(parts) + [vmem, smem],
        out_specs=(vmem, vmem),
        scratch_shapes=[pltpu.VMEM((2 * n_slabs, EX_DEV, LANES), jnp.float32)],
        name="vectors",
    )(*parts, segments, owner_map)


def fisher_kernel(scale, recv_ref, owner_ref, out_ref, stack, full):
    count, slabs = recv_ref.shape[0], recv_ref.shape[1]
    for i in range(count):
        for k in range(slabs):
            stack[pl.ds(i * EX_DEV, EX_DEV), pl.ds(k * LANES, LANES)] = recv_ref[i, k]
    product = lax.dot_general(
        stack[:, pl.ds(0, LANES)],
        stack[:, pl.ds(LANES, (slabs - 1) * LANES)],
        TN,
        precision=HIGHEST,
        preferred_element_type=jnp.float32,
    )
    own_rows = out_ref.shape[1]
    if own_rows == LANES:
        out_ref[0] = product * scale
    else:
        full[...] = product * scale
        start = (owner_ref[lax.axis_index("dp")] * own_rows) % LANES
        out_ref[0] = full[pl.ds(pl.multiple_of(start, own_rows), own_rows), :]


def fisher(recv, owner_map, own_rows):
    count, slabs = recv.shape[:2]
    col_width = (slabs - 1) * LANES
    return pl.pallas_call(
        functools.partial(fisher_kernel, 1.0 / (EX_DEV * count)),
        out_shape=jax.ShapeDtypeStruct((1, own_rows, col_width), jnp.float32),
        in_specs=[pl.BlockSpec(memory_space=pltpu.VMEM), pl.BlockSpec(memory_space=pltpu.SMEM)],
        out_specs=pl.BlockSpec(memory_space=pltpu.VMEM),
        scratch_shapes=[
            pltpu.VMEM((EX_DEV * count, slabs * LANES), jnp.float32),
            pltpu.VMEM((LANES, col_width), jnp.float32),
        ],
        name="fisher",
    )(recv, owner_map)


def shards(
    o_inputs,
    o_gradients,
    up_inputs,
    up_gradients,
    o_in_proj,
    o_out_proj,
    up_in_proj,
    up_out_proj,
    segment_ids,
    owner_map,
):
    tensor_count = lax.axis_size("tensor")
    dp_count = lax.axis_size("dp")
    width = o_in_proj.shape[1] * o_out_proj.shape[1]
    col_width = width // tensor_count
    own_rows = 2 * width // dp_count
    partial = project(
        (o_inputs, o_gradients, up_inputs, up_gradients),
        (o_in_proj.T, o_out_proj.T, up_in_proj.T, up_out_proj.T),
    )
    if tensor_count == 2:
        parts = (partial, lax.ppermute(partial, "tensor", [(0, 1), (1, 0)]))
    else:
        parts = (lax.psum(partial, "tensor"),)
    example_vectors, send = vectors(parts, segment_ids, owner_map, col_width, own_rows, dp_count)
    recv = lax.all_to_all(send, "dp", 0, 0, tiled=True)
    return example_vectors, fisher(recv, owner_map, own_rows)


def solution(mesh):
    in_specs = (
        P("dp", "tensor"),
        P("dp", "tensor"),
        P("dp", "tensor"),
        P("dp", "tensor"),
        P("tensor", None),
        P("tensor", None),
        P("tensor", None),
        P("tensor", None),
        P("dp", None),
        P(),
    )
    out_specs = (P(None, "dp", "tensor"), P("dp", None, "tensor"))
    return jax.shard_map(shards, mesh=mesh, in_specs=in_specs, out_specs=out_specs, check_vma=False)
```

```python
import functools

import jax
import jax.numpy as jnp
from jax import lax
from jax.experimental import pallas as pl
from jax.experimental.pallas import tpu as pltpu
from jax.sharding import PartitionSpec as P

TOK_DEV = 256
EX_DEV = 4
LANES = 128
NT = (((1,), (1,)), ((), ()))
TN = (((0,), (0,)), ((), ()))
VMEM_BYTES = 60 * 2**20
SMALL_BYTES = 8 * 2**20


def chunk_plan(widths):
    plan = []
    for which in sorted(range(len(widths)), key=lambda i: -widths[i]):
        start = 0
        while start < widths[which]:
            left = widths[which] - start
            size = left if left <= 6144 else 4096
            plan.append((which, start, size))
            start += size
    return plan


def split(x):
    high = x.astype(jnp.bfloat16)
    return high, (x - high.astype(jnp.float32)).astype(jnp.bfloat16)


def project_kernel(plan, halves, *refs):
    x_hbm, w_hbm, outs = refs[0:4], refs[4:8], refs[8:9]
    x_vmem, w_vmem, x_sem, w_sem = refs[9:13], refs[13:17], refs[17], refs[18]
    w_copies = [pltpu.make_async_copy(w_hbm[i], w_vmem[i], w_sem.at[i]) for i in range(4)]
    x_copies = [
        pltpu.make_async_copy(
            x_hbm[i].at[:, pl.ds(start, size)], x_vmem[i].at[:, pl.ds(start, size)], x_sem.at[n]
        )
        for n, (i, start, size) in enumerate(plan)
    ]
    for n, (i, start, size) in enumerate(plan):
        if start == 0:
            w_copies[i].start()
        x_copies[n].start()
    tokens, rank = x_vmem[0].shape[0], w_vmem[0].shape[0]
    part = tokens // halves
    totals = {}
    for n, (i, start, size) in enumerate(plan):
        if start == 0:
            w_copies[i].wait()
        x_copies[n].wait()
        w = w_vmem[i][:, pl.ds(start, size)]
        for h in range(halves):
            x = x_vmem[i][pl.ds(h * part, part), pl.ds(start, size)]
            product = lax.dot_general(x, w, NT, preferred_element_type=jnp.float32)
            totals[i, h] = product if start == 0 else totals[i, h] + product
    for i in range(4):
        for h in range(halves):
            low = totals[i, h].T
            for out in outs:
                out[h, pl.ds(i * rank, rank), :] = low


def project(xs, ws):
    plan = chunk_plan([x.shape[1] for x in xs])
    tokens, rank = xs[0].shape[0], ws[0].shape[0]
    halves = tokens // LANES
    low = jax.ShapeDtypeStruct((halves, 4 * rank, LANES), jnp.float32)
    return pl.pallas_call(
        functools.partial(project_kernel, plan, halves),
        out_shape=(low,),
        in_specs=[pl.BlockSpec(memory_space=pl.ANY)] * 8,
        out_specs=(pl.BlockSpec(memory_space=pltpu.VMEM),),
        scratch_shapes=[pltpu.VMEM(x.shape, x.dtype) for x in xs]
        + [pltpu.VMEM(w.shape, w.dtype) for w in ws]
        + [pltpu.SemaphoreType.DMA((len(plan),)), pltpu.SemaphoreType.DMA((4,))],
        compiler_params=pltpu.CompilerParams(vmem_limit_bytes=VMEM_BYTES),
        name="project",
    )(*xs, *ws)


def stage_kernel(low_ref, out_ref):
    out_ref[...] = low_ref[...]


def stage(low):
    return pl.pallas_call(
        stage_kernel,
        out_shape=jax.ShapeDtypeStruct(low.shape, low.dtype),
        in_specs=[pl.BlockSpec(memory_space=pltpu.VMEM)],
        out_specs=pl.BlockSpec(memory_space=pltpu.VMEM),
        compiler_params=pltpu.CompilerParams(vmem_limit_bytes=SMALL_BYTES),
        name="stage",
    )(low)


def vectors_kernel(n_parts, own_rows, *refs):
    parts, seg_ref, owner_ref, vec_ref, send_ref, slabs = refs[:n_parts], *refs[n_parts:]
    halves, rank = parts[0].shape[0], parts[0].shape[1] // 4
    fold = LANES // rank
    n_slabs = rank // fold
    col_slabs = vec_ref.shape[2] // LANES
    seg = seg_ref[...]
    lane = lax.broadcasted_iota(jnp.int32, (EX_DEV * n_slabs, LANES), 1)
    scale = (EX_DEV / TOK_DEV) ** 0.5

    def total(index):
        sums = [functools.reduce(lambda a, b: a + b, [part[h, index, :] for part in parts]) for h in range(halves)]
        return jnp.concatenate(sums, axis=1)

    for p in range(2):
        in_high, in_low = split(total(pl.ds(2 * p * rank, rank)))
        in_wide = jnp.concatenate([in_high, in_low, in_high], axis=1)
        in_wide = jnp.concatenate([in_wide] * fold, axis=0)
        rows = []
        for b in range(fold):
            out_rows = total(pl.ds((2 * p + 1) * rank + b, n_slabs, stride=fold))
            rows += [jnp.where(seg == e, out_rows, 0.0) for e in range(EX_DEV)]
        out_high, out_low = split(jnp.concatenate(rows, axis=0))
        out_wide = jnp.concatenate([out_high, out_high, out_low], axis=1)
        outer = lax.dot_general(out_wide, in_wide, NT, preferred_element_type=jnp.float32)
        flat = outer[: EX_DEV * n_slabs]
        for b in range(1, fold):
            block = outer[b * EX_DEV * n_slabs : (b + 1) * EX_DEV * n_slabs]
            flat = jnp.where(lane // rank == b, block, flat)
        flat = flat * scale
        for g in range(n_slabs):
            slabs[p * n_slabs + g] = jnp.concatenate(
                [flat[e * n_slabs + g : e * n_slabs + g + 1] for e in range(EX_DEV)], axis=0
            )
    t = lax.axis_index("tensor")
    for p in range(2):
        for k in range(col_slabs):
            vec_ref[p, :, pl.ds(k * LANES, LANES)] = slabs[p * n_slabs + t * col_slabs + k]
    for j in range(send_ref.shape[0]):
        first_row = owner_ref[j] * own_rows
        p = first_row // (rank * rank)
        send_ref[j, 0] = slabs[first_row // LANES]
        for k in range(col_slabs):
            send_ref[j, 1 + k] = slabs[p * n_slabs + t * col_slabs + k]


def vectors(parts, segments, owner_map, col_width, own_rows, dp_count):
    n_slabs = (parts[0].shape[1] // 4) ** 2 // LANES
    vmem, smem = pl.BlockSpec(memory_space=pltpu.VMEM), pl.BlockSpec(memory_space=pltpu.SMEM)
    return pl.pallas_call(
        functools.partial(vectors_kernel, len(parts), own_rows),
        out_shape=(
            jax.ShapeDtypeStruct((2, EX_DEV, col_width), jnp.float32),
            jax.ShapeDtypeStruct((dp_count, 1 + col_width // LANES, EX_DEV, LANES), jnp.float32),
        ),
        in_specs=[vmem] * len(parts) + [vmem, smem],
        out_specs=(vmem, vmem),
        scratch_shapes=[pltpu.VMEM((2 * n_slabs, EX_DEV, LANES), jnp.float32)],
        compiler_params=pltpu.CompilerParams(vmem_limit_bytes=SMALL_BYTES),
        name="vectors",
    )(*parts, segments, owner_map)


def fisher_kernel(scale, recv_ref, vec_ref, owner_ref, out_ref, vec_out, stack, full, sems):
    store = pltpu.make_async_copy(vec_ref, vec_out, sems.at[0])
    store.start()
    count, slabs = recv_ref.shape[0], recv_ref.shape[1]
    for i in range(count):
        for k in range(slabs):
            stack[pl.ds(i * EX_DEV, EX_DEV), pl.ds(k * LANES, LANES)] = recv_ref[i, k]
    own_rows, col_width = out_ref.shape[1:]
    start = 0
    if own_rows < LANES:
        start = (owner_ref[lax.axis_index("dp")] * own_rows) % LANES
        start = pl.multiple_of(start, own_rows)
    row_high, row_low = split(stack[:, pl.ds(0, LANES)])
    row_wide = jnp.concatenate([row_high, row_high, row_low], axis=0)
    pieces = 2 if col_width % (2 * LANES) == 0 else 1
    size = col_width // pieces
    stores = [store]
    for c in range(pieces):
        col_high, col_low = split(stack[:, pl.ds(LANES + c * size, size)])
        col_wide = jnp.concatenate([col_high, col_low, col_high], axis=0)
        product = lax.dot_general(row_wide, col_wide, TN, preferred_element_type=jnp.float32)
        full[:, pl.ds(c * size, size)] = product * scale
        stores.append(
            pltpu.make_async_copy(
                full.at[pl.ds(start, own_rows), pl.ds(c * size, size)],
                out_ref.at[0, :, pl.ds(c * size, size)],
                sems.at[1 + c],
            )
        )
        stores[-1].start()
    for store in stores:
        store.wait()


def fisher(recv, vec, owner_map, own_rows):
    count, slabs = recv.shape[:2]
    col_width = (slabs - 1) * LANES
    hbm = pl.BlockSpec(memory_space=pl.ANY)
    return pl.pallas_call(
        functools.partial(fisher_kernel, 1.0 / (EX_DEV * count)),
        out_shape=(
            jax.ShapeDtypeStruct((1, own_rows, col_width), jnp.float32),
            jax.ShapeDtypeStruct(vec.shape, vec.dtype),
        ),
        in_specs=[pl.BlockSpec(memory_space=pltpu.VMEM), hbm, pl.BlockSpec(memory_space=pltpu.SMEM)],
        out_specs=(hbm, hbm),
        scratch_shapes=[
            pltpu.VMEM((EX_DEV * count, slabs * LANES), jnp.float32),
            pltpu.VMEM((LANES, col_width), jnp.float32),
            pltpu.SemaphoreType.DMA((3,)),
        ],
        compiler_params=pltpu.CompilerParams(vmem_limit_bytes=SMALL_BYTES),
        name="fisher",
    )(recv, vec, owner_map)


def shards(
    o_inputs,
    o_gradients,
    up_inputs,
    up_gradients,
    o_in_proj,
    o_out_proj,
    up_in_proj,
    up_out_proj,
    segment_ids,
    owner_map,
):
    tensor_count = lax.axis_size("tensor")
    dp_count = lax.axis_size("dp")
    width = o_in_proj.shape[1] * o_out_proj.shape[1]
    col_width = width // tensor_count
    own_rows = 2 * width // dp_count
    (own,) = project(
        (o_inputs, o_gradients, up_inputs, up_gradients),
        (o_in_proj.T, o_out_proj.T, up_in_proj.T, up_out_proj.T),
    )
    if tensor_count == 2:
        parts = (stage(own), lax.ppermute(own, "tensor", [(0, 1), (1, 0)]))
    else:
        parts = (lax.psum(own, "tensor"),)
    vec, send = vectors(parts, segment_ids, owner_map, col_width, own_rows, dp_count)
    recv = lax.all_to_all(send, "dp", 0, 0, tiled=True)
    fisher_block, example_vectors = fisher(recv, vec, owner_map, own_rows)
    return example_vectors, fisher_block


def solution(mesh):
    in_specs = (
        P("dp", "tensor"),
        P("dp", "tensor"),
        P("dp", "tensor"),
        P("dp", "tensor"),
        P("tensor", None),
        P("tensor", None),
        P("tensor", None),
        P("tensor", None),
        P("dp", None),
        P(),
    )
    out_specs = (P(None, "dp", "tensor"), P("dp", None, "tensor"))
    return jax.shard_map(shards, mesh=mesh, in_specs=in_specs, out_specs=out_specs, check_vma=False)
```

```python
import functools

import jax
import jax.numpy as jnp
from jax import lax
from jax.experimental import pallas as pl
from jax.experimental.pallas import tpu as pltpu
from jax.sharding import PartitionSpec as P

TOK_DEV = 256
EX_DEV = 4
LANES = 128
NT = (((1,), (1,)), ((), ()))
TN = (((0,), (0,)), ((), ()))
PIECE = 4096
VMEM_BYTES = 60 * 2**20
SMALL_BYTES = 8 * 2**20


def chunk_plan(widths):
    plan = []
    for which in sorted(range(len(widths)), key=lambda i: -widths[i]):
        start = 0
        while start < widths[which]:
            size = (widths[which] - start) % PIECE or PIECE
            plan.append((which, start, size))
            start += size
    return plan


def split(x):
    high = x.astype(jnp.bfloat16)
    return high, (x - high.astype(jnp.float32)).astype(jnp.bfloat16)


def project_kernel(plan, halves, *refs):
    x_hbm, w_hbm, outs = refs[0:4], refs[4:8], refs[8:9]
    x_vmem, w_vmem, x_sem, w_sem = refs[9:13], refs[13:17], refs[17], refs[18]
    w_copies, x_copies = [], []
    for n, (i, start, size) in enumerate(plan):
        piece = (slice(None), pl.ds(start, size))
        w_copies.append(pltpu.make_async_copy(w_hbm[i].at[piece], w_vmem[i].at[piece], w_sem.at[n]))
        x_copies.append(pltpu.make_async_copy(x_hbm[i].at[piece], x_vmem[i].at[piece], x_sem.at[n]))
        w_copies[n].start()
        x_copies[n].start()
    tokens, rank = x_vmem[0].shape[0], w_vmem[0].shape[0]
    part = tokens // halves
    totals = {}
    for n, (i, start, size) in enumerate(plan):
        w_copies[n].wait()
        x_copies[n].wait()
        w = w_vmem[i][:, pl.ds(start, size)]
        for h in range(halves):
            x = x_vmem[i][pl.ds(h * part, part), pl.ds(start, size)]
            product = lax.dot_general(x, w, NT, preferred_element_type=jnp.float32)
            totals[i, h] = product if start == 0 else totals[i, h] + product
    for i in range(4):
        for h in range(halves):
            low = totals[i, h].T
            for out in outs:
                out[h, pl.ds(i * rank, rank), :] = low


def project(xs, ws):
    plan = chunk_plan([x.shape[1] for x in xs])
    tokens, rank = xs[0].shape[0], ws[0].shape[0]
    halves = tokens // LANES
    low = jax.ShapeDtypeStruct((halves, 4 * rank, LANES), jnp.float32)
    return pl.pallas_call(
        functools.partial(project_kernel, plan, halves),
        out_shape=(low,),
        in_specs=[pl.BlockSpec(memory_space=pl.ANY)] * 8,
        out_specs=(pl.BlockSpec(memory_space=pltpu.VMEM),),
        scratch_shapes=[pltpu.VMEM(x.shape, x.dtype) for x in xs]
        + [pltpu.VMEM(w.shape, w.dtype) for w in ws]
        + [pltpu.SemaphoreType.DMA((len(plan),))] * 2,
        compiler_params=pltpu.CompilerParams(vmem_limit_bytes=VMEM_BYTES),
        name="project",
    )(*xs, *ws)


def stage_kernel(low_ref, out_ref):
    out_ref[...] = low_ref[...]


def stage(low):
    return pl.pallas_call(
        stage_kernel,
        out_shape=jax.ShapeDtypeStruct(low.shape, low.dtype),
        in_specs=[pl.BlockSpec(memory_space=pltpu.VMEM)],
        out_specs=pl.BlockSpec(memory_space=pltpu.VMEM),
        compiler_params=pltpu.CompilerParams(vmem_limit_bytes=SMALL_BYTES),
        name="stage",
    )(low)


def vectors_kernel(n_parts, own_rows, *refs):
    parts, seg_ref, owner_in, vec_ref, send_ref, slabs, owner_ref, sem = refs[:n_parts], *refs[n_parts:]
    owner_copy = pltpu.make_async_copy(owner_in, owner_ref, sem)
    owner_copy.start()
    halves, rank = parts[0].shape[0], parts[0].shape[1] // 4
    fold = LANES // rank
    n_slabs = rank // fold
    col_slabs = vec_ref.shape[2] // LANES
    seg = seg_ref[...]
    lane = lax.broadcasted_iota(jnp.int32, (EX_DEV * n_slabs, LANES), 1)
    scale = (EX_DEV / TOK_DEV) ** 0.5

    def total(index):
        sums = [functools.reduce(lambda a, b: a + b, [part[h, index, :] for part in parts]) for h in range(halves)]
        return jnp.concatenate(sums, axis=1)

    for p in range(2):
        in_high, in_low = split(total(pl.ds(2 * p * rank, rank)))
        in_wide = jnp.concatenate([in_high, in_low, in_high], axis=1)
        in_wide = jnp.concatenate([in_wide] * fold, axis=0)
        rows = []
        for b in range(fold):
            out_rows = total(pl.ds((2 * p + 1) * rank + b, n_slabs, stride=fold))
            rows += [jnp.where(seg == e, out_rows, 0.0) for e in range(EX_DEV)]
        out_high, out_low = split(jnp.concatenate(rows, axis=0))
        out_wide = jnp.concatenate([out_high, out_high, out_low], axis=1)
        outer = lax.dot_general(out_wide, in_wide, NT, preferred_element_type=jnp.float32)
        flat = outer[: EX_DEV * n_slabs]
        for b in range(1, fold):
            block = outer[b * EX_DEV * n_slabs : (b + 1) * EX_DEV * n_slabs]
            flat = jnp.where(lane // rank == b, block, flat)
        flat = flat * scale
        for g in range(n_slabs):
            slabs[p * n_slabs + g] = jnp.concatenate(
                [flat[e * n_slabs + g : e * n_slabs + g + 1] for e in range(EX_DEV)], axis=0
            )
    t = lax.axis_index("tensor")
    for p in range(2):
        for k in range(col_slabs):
            vec_ref[p, :, pl.ds(k * LANES, LANES)] = slabs[p * n_slabs + t * col_slabs + k]
    owner_copy.wait()
    for j in range(send_ref.shape[0]):
        first_row = owner_ref[j] * own_rows
        p = first_row // (rank * rank)
        send_ref[j, 0] = slabs[first_row // LANES]
        for k in range(col_slabs):
            send_ref[j, 1 + k] = slabs[p * n_slabs + t * col_slabs + k]


def vectors(parts, segments, owner_map, col_width, own_rows, dp_count):
    n_slabs = (parts[0].shape[1] // 4) ** 2 // LANES
    vmem = pl.BlockSpec(memory_space=pltpu.VMEM)
    return pl.pallas_call(
        functools.partial(vectors_kernel, len(parts), own_rows),
        out_shape=(
            jax.ShapeDtypeStruct((2, EX_DEV, col_width), jnp.float32),
            jax.ShapeDtypeStruct((dp_count, 1 + col_width // LANES, EX_DEV, LANES), jnp.float32),
        ),
        in_specs=[vmem] * len(parts) + [vmem, pl.BlockSpec(memory_space=pl.ANY)],
        out_specs=(vmem, vmem),
        scratch_shapes=[
            pltpu.VMEM((2 * n_slabs, EX_DEV, LANES), jnp.float32),
            pltpu.SMEM(owner_map.shape, owner_map.dtype),
            pltpu.SemaphoreType.DMA,
        ],
        compiler_params=pltpu.CompilerParams(vmem_limit_bytes=SMALL_BYTES),
        name="vectors",
    )(*parts, segments, owner_map)


def fisher_kernel(scale, recv_ref, vec_ref, *refs):
    out_ref, vec_out, stack, full, sems = refs[-5:]
    store = pltpu.make_async_copy(vec_ref, vec_out, sems.at[0])
    store.start()
    count, slabs = recv_ref.shape[0], recv_ref.shape[1]
    for i in range(count):
        for k in range(slabs):
            stack[pl.ds(i * EX_DEV, EX_DEV), pl.ds(k * LANES, LANES)] = recv_ref[i, k]
    own_rows, col_width = out_ref.shape[1:]
    start = 0
    if own_rows < LANES:
        start = (refs[0][lax.axis_index("dp")] * own_rows) % LANES
        start = pl.multiple_of(start, own_rows)
    row_high, row_low = split(stack[:, pl.ds(0, LANES)])
    row_wide = jnp.concatenate([row_high, row_high, row_low], axis=0)
    pieces = 2 if col_width % (2 * LANES) == 0 else 1
    size = col_width // pieces
    stores = [store]
    for c in range(pieces):
        col_high, col_low = split(stack[:, pl.ds(LANES + c * size, size)])
        col_wide = jnp.concatenate([col_high, col_low, col_high], axis=0)
        product = lax.dot_general(row_wide, col_wide, TN, preferred_element_type=jnp.float32)
        full[:, pl.ds(c * size, size)] = product * scale
        stores.append(
            pltpu.make_async_copy(
                full.at[pl.ds(start, own_rows), pl.ds(c * size, size)],
                out_ref.at[0, :, pl.ds(c * size, size)],
                sems.at[1 + c],
            )
        )
        stores[-1].start()
    for store in stores:
        store.wait()


def fisher(recv, vec, owner_map, own_rows):
    count, slabs = recv.shape[:2]
    col_width = (slabs - 1) * LANES
    hbm = pl.BlockSpec(memory_space=pl.ANY)
    owners = (owner_map,) if own_rows < LANES else ()
    return pl.pallas_call(
        functools.partial(fisher_kernel, 1.0 / (EX_DEV * count)),
        out_shape=(
            jax.ShapeDtypeStruct((1, own_rows, col_width), jnp.float32),
            jax.ShapeDtypeStruct(vec.shape, vec.dtype),
        ),
        in_specs=[pl.BlockSpec(memory_space=pltpu.VMEM), hbm]
        + [pl.BlockSpec(memory_space=pltpu.SMEM)] * len(owners),
        out_specs=(hbm, hbm),
        scratch_shapes=[
            pltpu.VMEM((EX_DEV * count, slabs * LANES), jnp.float32),
            pltpu.VMEM((LANES, col_width), jnp.float32),
            pltpu.SemaphoreType.DMA((3,)),
        ],
        compiler_params=pltpu.CompilerParams(vmem_limit_bytes=SMALL_BYTES),
        name="fisher",
    )(recv, vec, *owners)


def shards(
    o_inputs,
    o_gradients,
    up_inputs,
    up_gradients,
    o_in_proj,
    o_out_proj,
    up_in_proj,
    up_out_proj,
    segment_ids,
    owner_map,
):
    tensor_count = lax.axis_size("tensor")
    dp_count = lax.axis_size("dp")
    width = o_in_proj.shape[1] * o_out_proj.shape[1]
    col_width = width // tensor_count
    own_rows = 2 * width // dp_count
    (own,) = project(
        (o_inputs, o_gradients, up_inputs, up_gradients),
        (o_in_proj.T, o_out_proj.T, up_in_proj.T, up_out_proj.T),
    )
    if tensor_count == 2:
        parts = (stage(own), lax.ppermute(own, "tensor", [(0, 1), (1, 0)]))
    else:
        parts = (lax.psum(own, "tensor"),)
    vec, send = vectors(parts, segment_ids, owner_map, col_width, own_rows, dp_count)
    recv = lax.all_to_all(send, "dp", 0, 0, tiled=True)
    fisher_block, example_vectors = fisher(recv, vec, owner_map, own_rows)
    return example_vectors, fisher_block


def solution(mesh):
    in_specs = (
        P("dp", "tensor"),
        P("dp", "tensor"),
        P("dp", "tensor"),
        P("dp", "tensor"),
        P("tensor", None),
        P("tensor", None),
        P("tensor", None),
        P("tensor", None),
        P("dp", None),
        P(),
    )
    out_specs = (P(None, "dp", "tensor"), P("dp", None, "tensor"))
    return jax.shard_map(shards, mesh=mesh, in_specs=in_specs, out_specs=out_specs, check_vma=False)
```

```python
import functools

import jax
import jax.numpy as jnp
from jax import lax
from jax.experimental import pallas as pl
from jax.experimental.pallas import tpu as pltpu
from jax.sharding import PartitionSpec as P

TOK_DEV = 256
EX_DEV = 4
LANES = 128
NT = (((1,), (1,)), ((), ()))
TN = (((0,), (0,)), ((), ()))
PIECE = 4096
VMEM_BYTES = 54976 * 2**10
SMALL_BYTES = 8 * 2**20


def chunk_plan(widths):
    plan = []
    for which in sorted(range(len(widths)), key=lambda i: -widths[i]):
        start = 0
        while start < widths[which]:
            size = (widths[which] - start) % PIECE or PIECE
            plan.append((which, start, size))
            start += size
    return plan


def split(x):
    high = x.astype(jnp.bfloat16)
    return high, (x - high.astype(jnp.float32)).astype(jnp.bfloat16)


def project_kernel(plan, halves, *refs):
    x_hbm, w_hbm, outs = refs[0:4], refs[4:8], refs[8:9]
    x_vmem, w_vmem, x_sem, w_sem = refs[9:13], refs[13:17], refs[17], refs[18]
    w_copies, x_copies = [], []
    for n, (i, start, size) in enumerate(plan):
        piece = (slice(None), pl.ds(start, size))
        w_copies.append(pltpu.make_async_copy(w_hbm[i].at[piece], w_vmem[i].at[piece], w_sem.at[n]))
        x_copies.append(pltpu.make_async_copy(x_hbm[i].at[piece], x_vmem[i].at[piece], x_sem.at[n]))
        w_copies[n].start()
        x_copies[n].start()
    tokens, rank = x_vmem[0].shape[0], w_vmem[0].shape[0]
    part = tokens // halves
    totals = {}
    for n, (i, start, size) in enumerate(plan):
        w_copies[n].wait()
        x_copies[n].wait()
        w = w_vmem[i][:, pl.ds(start, size)]
        for h in range(halves):
            x = x_vmem[i][pl.ds(h * part, part), pl.ds(start, size)]
            product = lax.dot_general(x, w, NT, preferred_element_type=jnp.float32)
            totals[i, h] = product if start == 0 else totals[i, h] + product
    for i in range(4):
        for h in range(halves):
            low = totals[i, h].T
            for out in outs:
                out[h, pl.ds(i * rank, rank), :] = low


def project(xs, ws):
    plan = chunk_plan([x.shape[1] for x in xs])
    tokens, rank = xs[0].shape[0], ws[0].shape[0]
    halves = tokens // LANES
    low = jax.ShapeDtypeStruct((halves, 4 * rank, LANES), jnp.float32)
    return pl.pallas_call(
        functools.partial(project_kernel, plan, halves),
        out_shape=(low,),
        in_specs=[pl.BlockSpec(memory_space=pl.ANY)] * 8,
        out_specs=(pl.BlockSpec(memory_space=pltpu.VMEM),),
        scratch_shapes=[pltpu.VMEM(x.shape, x.dtype) for x in xs]
        + [pltpu.VMEM(w.shape, w.dtype) for w in ws]
        + [pltpu.SemaphoreType.DMA((len(plan),))] * 2,
        compiler_params=pltpu.CompilerParams(vmem_limit_bytes=VMEM_BYTES),
        name="project",
    )(*xs, *ws)


def stage_kernel(low_ref, out_ref):
    out_ref[...] = low_ref[...]


def stage(low):
    return pl.pallas_call(
        stage_kernel,
        out_shape=jax.ShapeDtypeStruct(low.shape, low.dtype),
        in_specs=[pl.BlockSpec(memory_space=pltpu.VMEM)],
        out_specs=pl.BlockSpec(memory_space=pltpu.VMEM),
        compiler_params=pltpu.CompilerParams(vmem_limit_bytes=SMALL_BYTES),
        name="stage",
    )(low)


def vectors_kernel(n_parts, own_rows, *refs):
    parts, seg_ref, owner_in, vec_ref, send_ref, slabs, owner_ref, sem = refs[:n_parts], *refs[n_parts:]
    owner_copy = pltpu.make_async_copy(owner_in, owner_ref, sem)
    owner_copy.start()
    halves, rank = parts[0].shape[0], parts[0].shape[1] // 4
    fold = LANES // rank
    n_slabs = rank // fold
    col_slabs = vec_ref.shape[2] // LANES
    seg = seg_ref[...]
    lane = lax.broadcasted_iota(jnp.int32, (EX_DEV * n_slabs, LANES), 1)
    scale = (EX_DEV / TOK_DEV) ** 0.5

    def total(index):
        sums = [functools.reduce(lambda a, b: a + b, [part[h, index, :] for part in parts]) for h in range(halves)]
        return jnp.concatenate(sums, axis=1)

    for p in range(2):
        in_high, in_low = split(total(pl.ds(2 * p * rank, rank)))
        in_wide = jnp.concatenate([in_high, in_low, in_high], axis=1)
        in_wide = jnp.concatenate([in_wide] * fold, axis=0)
        rows = []
        for b in range(fold):
            out_rows = total(pl.ds((2 * p + 1) * rank + b, n_slabs, stride=fold))
            rows += [jnp.where(seg == e, out_rows, 0.0) for e in range(EX_DEV)]
        out_high, out_low = split(jnp.concatenate(rows, axis=0))
        out_wide = jnp.concatenate([out_high, out_high, out_low], axis=1)
        outer = lax.dot_general(out_wide, in_wide, NT, preferred_element_type=jnp.float32)
        flat = outer[: EX_DEV * n_slabs]
        for b in range(1, fold):
            block = outer[b * EX_DEV * n_slabs : (b + 1) * EX_DEV * n_slabs]
            flat = jnp.where(lane // rank == b, block, flat)
        flat = flat * scale
        for g in range(n_slabs):
            slabs[p * n_slabs + g] = jnp.concatenate(
                [flat[e * n_slabs + g : e * n_slabs + g + 1] for e in range(EX_DEV)], axis=0
            )
    t = lax.axis_index("tensor")
    for p in range(2):
        for k in range(col_slabs):
            vec_ref[p, :, pl.ds(k * LANES, LANES)] = slabs[p * n_slabs + t * col_slabs + k]
    owner_copy.wait()
    for j in range(send_ref.shape[0]):
        first_row = owner_ref[j] * own_rows
        p = first_row // (rank * rank)
        send_ref[j, 0] = slabs[first_row // LANES]
        for k in range(col_slabs):
            send_ref[j, 1 + k] = slabs[p * n_slabs + t * col_slabs + k]


def vectors(parts, segments, owner_map, col_width, own_rows, dp_count):
    n_slabs = (parts[0].shape[1] // 4) ** 2 // LANES
    vmem = pl.BlockSpec(memory_space=pltpu.VMEM)
    return pl.pallas_call(
        functools.partial(vectors_kernel, len(parts), own_rows),
        out_shape=(
            jax.ShapeDtypeStruct((2, EX_DEV, col_width), jnp.float32),
            jax.ShapeDtypeStruct((dp_count, 1 + col_width // LANES, EX_DEV, LANES), jnp.float32),
        ),
        in_specs=[vmem] * len(parts) + [vmem, pl.BlockSpec(memory_space=pl.ANY)],
        out_specs=(vmem, vmem),
        scratch_shapes=[
            pltpu.VMEM((2 * n_slabs, EX_DEV, LANES), jnp.float32),
            pltpu.SMEM(owner_map.shape, owner_map.dtype),
            pltpu.SemaphoreType.DMA,
        ],
        compiler_params=pltpu.CompilerParams(vmem_limit_bytes=SMALL_BYTES),
        name="vectors",
    )(*parts, segments, owner_map)


def fisher_kernel(scale, recv_ref, vec_ref, *refs):
    out_ref, vec_out, stack, full, sems = refs[-5:]
    store = pltpu.make_async_copy(vec_ref, vec_out, sems.at[0])
    store.start()
    count, slabs = recv_ref.shape[0], recv_ref.shape[1]
    for i in range(count):
        for k in range(slabs):
            stack[pl.ds(i * EX_DEV, EX_DEV), pl.ds(k * LANES, LANES)] = recv_ref[i, k]
    own_rows, col_width = out_ref.shape[1:]
    start = 0
    if own_rows < LANES:
        start = (refs[0][lax.axis_index("dp")] * own_rows) % LANES
        start = pl.multiple_of(start, own_rows)
    row_high, row_low = split(stack[:, pl.ds(0, LANES)])
    row_wide = jnp.concatenate([row_high, row_high, row_low], axis=0)
    pieces = 2 if col_width % (2 * LANES) == 0 else 1
    size = col_width // pieces
    stores = [store]
    for c in range(pieces):
        col_high, col_low = split(stack[:, pl.ds(LANES + c * size, size)])
        col_wide = jnp.concatenate([col_high, col_low, col_high], axis=0)
        product = lax.dot_general(row_wide, col_wide, TN, preferred_element_type=jnp.float32)
        full[:, pl.ds(c * size, size)] = product * scale
        stores.append(
            pltpu.make_async_copy(
                full.at[pl.ds(start, own_rows), pl.ds(c * size, size)],
                out_ref.at[0, :, pl.ds(c * size, size)],
                sems.at[1 + c],
            )
        )
        stores[-1].start()
    for store in stores:
        store.wait()


def fisher(recv, vec, owner_map, own_rows):
    count, slabs = recv.shape[:2]
    col_width = (slabs - 1) * LANES
    hbm = pl.BlockSpec(memory_space=pl.ANY)
    owners = (owner_map,) if own_rows < LANES else ()
    return pl.pallas_call(
        functools.partial(fisher_kernel, 1.0 / (EX_DEV * count)),
        out_shape=(
            jax.ShapeDtypeStruct((1, own_rows, col_width), jnp.float32),
            jax.ShapeDtypeStruct(vec.shape, vec.dtype),
        ),
        in_specs=[pl.BlockSpec(memory_space=pltpu.VMEM), hbm]
        + [pl.BlockSpec(memory_space=pltpu.SMEM)] * len(owners),
        out_specs=(hbm, hbm),
        scratch_shapes=[
            pltpu.VMEM((EX_DEV * count, slabs * LANES), jnp.float32),
            pltpu.VMEM((LANES, col_width), jnp.float32),
            pltpu.SemaphoreType.DMA((3,)),
        ],
        compiler_params=pltpu.CompilerParams(vmem_limit_bytes=SMALL_BYTES),
        name="fisher",
    )(recv, vec, *owners)


def shards(
    o_inputs,
    o_gradients,
    up_inputs,
    up_gradients,
    o_in_proj,
    o_out_proj,
    up_in_proj,
    up_out_proj,
    segment_ids,
    owner_map,
):
    tensor_count = lax.axis_size("tensor")
    dp_count = lax.axis_size("dp")
    width = o_in_proj.shape[1] * o_out_proj.shape[1]
    col_width = width // tensor_count
    own_rows = 2 * width // dp_count
    (own,) = project(
        (o_inputs, o_gradients, up_inputs, up_gradients),
        (o_in_proj.T, o_out_proj.T, up_in_proj.T, up_out_proj.T),
    )
    if tensor_count == 2:
        parts = (stage(own), lax.ppermute(own, "tensor", [(0, 1), (1, 0)]))
    else:
        parts = (lax.psum(own, "tensor"),)
    vec, send = vectors(parts, segment_ids, owner_map, col_width, own_rows, dp_count)
    recv = lax.all_to_all(send, "dp", 0, 0, tiled=True)
    fisher_block, example_vectors = fisher(recv, vec, owner_map, own_rows)
    return example_vectors, fisher_block


def solution(mesh):
    in_specs = (
        P("dp", "tensor"),
        P("dp", "tensor"),
        P("dp", "tensor"),
        P("dp", "tensor"),
        P("tensor", None),
        P("tensor", None),
        P("tensor", None),
        P("tensor", None),
        P("dp", None),
        P(),
    )
    out_specs = (P(None, "dp", "tensor"), P("dp", None, "tensor"))
    return jax.shard_map(shards, mesh=mesh, in_specs=in_specs, out_specs=out_specs, check_vma=False)
```

```python
import functools

import jax
import jax.numpy as jnp
from jax import lax
from jax.experimental import pallas as pl
from jax.experimental.pallas import tpu as pltpu
from jax.sharding import PartitionSpec as P

TOK_DEV = 256
EX_DEV = 4
LANES = 128
NT = (((1,), (1,)), ((), ()))
TN = (((0,), (0,)), ((), ()))
PIECE = 4096
VMEM_BYTES = 54976 * 2**10
SMALL_BYTES = 8 * 2**20


def chunk_plan(widths):
    plan = []
    for which in sorted(range(len(widths)), key=lambda i: -widths[i]):
        start = 0
        while start < widths[which]:
            size = (widths[which] - start) % PIECE or PIECE
            plan.append((which, start, size))
            start += size
    return plan


def split(x):
    high = x.astype(jnp.bfloat16)
    return high, (x - high.astype(jnp.float32)).astype(jnp.bfloat16)


def project_kernel(plan, halves, *refs):
    x_hbm, w_hbm, outs = refs[0:4], refs[4:8], refs[8:9]
    x_vmem, w_vmem, x_sem, w_sem = refs[9:13], refs[13:17], refs[17], refs[18]
    w_copies, x_copies = [], []
    for n, (i, start, size) in enumerate(plan):
        piece = (slice(None), pl.ds(start, size))
        w_copies.append(pltpu.make_async_copy(w_hbm[i].at[piece], w_vmem[i].at[piece], w_sem.at[n]))
        x_copies.append(pltpu.make_async_copy(x_hbm[i].at[piece], x_vmem[i].at[piece], x_sem.at[n]))
        w_copies[n].start()
        x_copies[n].start()
    tokens, rank = x_vmem[0].shape[0], w_vmem[0].shape[0]
    part = tokens // halves
    totals = {}
    for n, (i, start, size) in enumerate(plan):
        w_copies[n].wait()
        x_copies[n].wait()
        w = w_vmem[i][:, pl.ds(start, size)]
        for h in range(halves):
            x = x_vmem[i][pl.ds(h * part, part), pl.ds(start, size)]
            product = lax.dot_general(x, w, NT, preferred_element_type=jnp.float32)
            totals[i, h] = product if start == 0 else totals[i, h] + product
    for i in range(4):
        for h in range(halves):
            low = totals[i, h].T
            for out in outs:
                out[h, pl.ds(i * rank, rank), :] = low


def project(xs, ws):
    plan = chunk_plan([x.shape[1] for x in xs])
    tokens, rank = xs[0].shape[0], ws[0].shape[0]
    halves = tokens // LANES
    low = jax.ShapeDtypeStruct((halves, 4 * rank, LANES), jnp.float32)
    return pl.pallas_call(
        functools.partial(project_kernel, plan, halves),
        out_shape=(low,),
        in_specs=[pl.BlockSpec(memory_space=pl.ANY)] * 8,
        out_specs=(pl.BlockSpec(memory_space=pltpu.VMEM),),
        scratch_shapes=[pltpu.VMEM(x.shape, x.dtype) for x in xs]
        + [pltpu.VMEM(w.shape, w.dtype) for w in ws]
        + [pltpu.SemaphoreType.DMA((len(plan),))] * 2,
        compiler_params=pltpu.CompilerParams(vmem_limit_bytes=VMEM_BYTES),
        name="project",
    )(*xs, *ws)


def stage_kernel(low_ref, out_ref):
    out_ref[...] = low_ref[...]


def stage(low):
    return pl.pallas_call(
        stage_kernel,
        out_shape=jax.ShapeDtypeStruct(low.shape, low.dtype),
        in_specs=[pl.BlockSpec(memory_space=pltpu.VMEM)],
        out_specs=pl.BlockSpec(memory_space=pltpu.VMEM),
        compiler_params=pltpu.CompilerParams(vmem_limit_bytes=SMALL_BYTES),
        name="stage",
    )(low)


def vectors_kernel(n_parts, *refs):
    parts, seg_ref, wanted_ref, vec_ref, send_ref, slabs = refs[:n_parts], *refs[n_parts:]
    halves, rank = parts[0].shape[0], parts[0].shape[1] // 4
    fold = LANES // rank
    n_slabs = rank // fold
    col_slabs = vec_ref.shape[2] // LANES
    seg = seg_ref[...]
    lane = lax.broadcasted_iota(jnp.int32, (EX_DEV * n_slabs, LANES), 1)
    scale = (EX_DEV / TOK_DEV) ** 0.5

    def total(index):
        sums = [functools.reduce(lambda a, b: a + b, [part[h, index, :] for part in parts]) for h in range(halves)]
        return jnp.concatenate(sums, axis=1)

    for p in range(2):
        in_high, in_low = split(total(pl.ds(2 * p * rank, rank)))
        in_wide = jnp.concatenate([in_high, in_low, in_high], axis=1)
        in_wide = jnp.concatenate([in_wide] * fold, axis=0)
        rows = []
        for b in range(fold):
            out_rows = total(pl.ds((2 * p + 1) * rank + b, n_slabs, stride=fold))
            rows += [jnp.where(seg == e, out_rows, 0.0) for e in range(EX_DEV)]
        out_high, out_low = split(jnp.concatenate(rows, axis=0))
        out_wide = jnp.concatenate([out_high, out_high, out_low], axis=1)
        outer = lax.dot_general(out_wide, in_wide, NT, preferred_element_type=jnp.float32)
        flat = outer[: EX_DEV * n_slabs]
        for b in range(1, fold):
            block = outer[b * EX_DEV * n_slabs : (b + 1) * EX_DEV * n_slabs]
            flat = jnp.where(lane // rank == b, block, flat)
        flat = flat * scale
        for g in range(n_slabs):
            slabs[p * n_slabs + g] = jnp.concatenate(
                [flat[e * n_slabs + g : e * n_slabs + g + 1] for e in range(EX_DEV)], axis=0
            )
    t = lax.axis_index("tensor")
    columns = [[slabs[p * n_slabs + t * col_slabs + k] for k in range(col_slabs)] for p in range(2)]
    for p in range(2):
        for k in range(col_slabs):
            vec_ref[p, :, pl.ds(k * LANES, LANES)] = columns[p][k]
    rows = [slabs[s] for s in range(2 * n_slabs)]
    for j in range(send_ref.shape[0]):
        wanted = wanted_ref[j]
        row_slab = rows[0]
        for s in range(1, 2 * n_slabs):
            row_slab = jnp.where(wanted == s, rows[s], row_slab)
        send_ref[j, 0] = row_slab
        for k in range(col_slabs):
            send_ref[j, 1 + k] = jnp.where(wanted < n_slabs, columns[0][k], columns[1][k])


def vectors(parts, segments, wanted, col_width):
    n_slabs = (parts[0].shape[1] // 4) ** 2 // LANES
    vmem = pl.BlockSpec(memory_space=pltpu.VMEM)
    return pl.pallas_call(
        functools.partial(vectors_kernel, len(parts)),
        out_shape=(
            jax.ShapeDtypeStruct((2, EX_DEV, col_width), jnp.float32),
            jax.ShapeDtypeStruct((wanted.shape[0], 1 + col_width // LANES, EX_DEV, LANES), jnp.float32),
        ),
        in_specs=[vmem] * (len(parts) + 2),
        out_specs=(vmem, vmem),
        scratch_shapes=[pltpu.VMEM((2 * n_slabs, EX_DEV, LANES), jnp.float32)],
        compiler_params=pltpu.CompilerParams(vmem_limit_bytes=SMALL_BYTES),
        name="vectors",
    )(*parts, segments, wanted)


def fisher_kernel(scale, recv_ref, vec_ref, *refs):
    out_ref, vec_out, stack, full, sems = refs[-5:]
    store = pltpu.make_async_copy(vec_ref, vec_out, sems.at[0])
    store.start()
    count, slabs = recv_ref.shape[0], recv_ref.shape[1]
    for i in range(count):
        for k in range(slabs):
            stack[pl.ds(i * EX_DEV, EX_DEV), pl.ds(k * LANES, LANES)] = recv_ref[i, k]
    own_rows, col_width = out_ref.shape[1:]
    start = 0
    if own_rows < LANES:
        start = (refs[0][lax.axis_index("dp")] * own_rows) % LANES
        start = pl.multiple_of(start, own_rows)
    row_high, row_low = split(stack[:, pl.ds(0, LANES)])
    row_wide = jnp.concatenate([row_high, row_high, row_low], axis=0)
    pieces = 2 if col_width % (2 * LANES) == 0 else 1
    size = col_width // pieces
    stores = [store]
    for c in range(pieces):
        col_high, col_low = split(stack[:, pl.ds(LANES + c * size, size)])
        col_wide = jnp.concatenate([col_high, col_low, col_high], axis=0)
        product = lax.dot_general(row_wide, col_wide, TN, preferred_element_type=jnp.float32)
        full[:, pl.ds(c * size, size)] = product * scale
        stores.append(
            pltpu.make_async_copy(
                full.at[pl.ds(start, own_rows), pl.ds(c * size, size)],
                out_ref.at[0, :, pl.ds(c * size, size)],
                sems.at[1 + c],
            )
        )
        stores[-1].start()
    for store in stores:
        store.wait()


def fisher(recv, vec, owner_map, own_rows):
    count, slabs = recv.shape[:2]
    col_width = (slabs - 1) * LANES
    hbm = pl.BlockSpec(memory_space=pl.ANY)
    owners = (owner_map,) if own_rows < LANES else ()
    return pl.pallas_call(
        functools.partial(fisher_kernel, 1.0 / (EX_DEV * count)),
        out_shape=(
            jax.ShapeDtypeStruct((1, own_rows, col_width), jnp.float32),
            jax.ShapeDtypeStruct(vec.shape, vec.dtype),
        ),
        in_specs=[pl.BlockSpec(memory_space=pltpu.VMEM), hbm]
        + [pl.BlockSpec(memory_space=pltpu.SMEM)] * len(owners),
        out_specs=(hbm, hbm),
        scratch_shapes=[
            pltpu.VMEM((EX_DEV * count, slabs * LANES), jnp.float32),
            pltpu.VMEM((LANES, col_width), jnp.float32),
            pltpu.SemaphoreType.DMA((3,)),
        ],
        compiler_params=pltpu.CompilerParams(vmem_limit_bytes=SMALL_BYTES),
        name="fisher",
    )(recv, vec, *owners)


def shards(
    o_inputs,
    o_gradients,
    up_inputs,
    up_gradients,
    o_in_proj,
    o_out_proj,
    up_in_proj,
    up_out_proj,
    segment_ids,
    owner_map,
):
    tensor_count = lax.axis_size("tensor")
    dp_count = lax.axis_size("dp")
    width = o_in_proj.shape[1] * o_out_proj.shape[1]
    col_width = width // tensor_count
    own_rows = 2 * width // dp_count
    (own,) = project(
        (o_inputs, o_gradients, up_inputs, up_gradients),
        (o_in_proj.T, o_out_proj.T, up_in_proj.T, up_out_proj.T),
    )
    if tensor_count == 2:
        parts = (stage(own), lax.ppermute(own, "tensor", [(0, 1), (1, 0)]))
    else:
        parts = (lax.psum(own, "tensor"),)
    wanted = jnp.broadcast_to((owner_map * own_rows // LANES)[:, None, None], (dp_count, EX_DEV, LANES))
    vec, send = vectors(parts, segment_ids, wanted, col_width)
    recv = lax.all_to_all(send, "dp", 0, 0, tiled=True)
    fisher_block, example_vectors = fisher(recv, vec, owner_map, own_rows)
    return example_vectors, fisher_block


def solution(mesh):
    in_specs = (
        P("dp", "tensor"),
        P("dp", "tensor"),
        P("dp", "tensor"),
        P("dp", "tensor"),
        P("tensor", None),
        P("tensor", None),
        P("tensor", None),
        P("tensor", None),
        P("dp", None),
        P(),
    )
    out_specs = (P(None, "dp", "tensor"), P("dp", None, "tensor"))
    return jax.shard_map(shards, mesh=mesh, in_specs=in_specs, out_specs=out_specs, check_vma=False)
```

```python
import functools

import jax
import jax.numpy as jnp
from jax import lax
from jax.experimental import pallas as pl
from jax.experimental.pallas import tpu as pltpu
from jax.sharding import PartitionSpec as P

TOK_DEV = 256
EX_DEV = 4
LANES = 128
NT = (((1,), (1,)), ((), ()))
TN = (((0,), (0,)), ((), ()))
PIECE = 4096
PLANE = 4
PLANE_SHIFTS = (2, 1, 3)
PLANE_STEPS = (2, 3, 1)
VMEM_BYTES = 54976 * 2**10
SMALL_BYTES = 8 * 2**20


def chunk_plan(widths):
    plan = []
    for which in sorted(range(len(widths)), key=lambda i: -widths[i]):
        start = 0
        while start < widths[which]:
            size = (widths[which] - start) % PIECE or PIECE
            plan.append((which, start, size))
            start += size
    return plan


def split(x):
    high = x.astype(jnp.bfloat16)
    return high, (x - high.astype(jnp.float32)).astype(jnp.bfloat16)


def project_kernel(plan, halves, *refs):
    x_hbm, w_hbm, outs = refs[0:4], refs[4:8], refs[8:9]
    x_vmem, w_vmem, x_sem, w_sem = refs[9:13], refs[13:17], refs[17], refs[18]
    w_copies, x_copies = [], []
    for n, (i, start, size) in enumerate(plan):
        piece = (slice(None), pl.ds(start, size))
        w_copies.append(pltpu.make_async_copy(w_hbm[i].at[piece], w_vmem[i].at[piece], w_sem.at[n]))
        x_copies.append(pltpu.make_async_copy(x_hbm[i].at[piece], x_vmem[i].at[piece], x_sem.at[n]))
        w_copies[n].start()
        x_copies[n].start()
    tokens, rank = x_vmem[0].shape[0], w_vmem[0].shape[0]
    part = tokens // halves
    totals = {}
    for n, (i, start, size) in enumerate(plan):
        w_copies[n].wait()
        x_copies[n].wait()
        w = w_vmem[i][:, pl.ds(start, size)]
        for h in range(halves):
            x = x_vmem[i][pl.ds(h * part, part), pl.ds(start, size)]
            product = lax.dot_general(x, w, NT, preferred_element_type=jnp.float32)
            totals[i, h] = product if start == 0 else totals[i, h] + product
    for i in range(4):
        for h in range(halves):
            low = totals[i, h].T
            for out in outs:
                out[h, pl.ds(i * rank, rank), :] = low


def project(xs, ws):
    plan = chunk_plan([x.shape[1] for x in xs])
    tokens, rank = xs[0].shape[0], ws[0].shape[0]
    halves = tokens // LANES
    low = jax.ShapeDtypeStruct((halves, 4 * rank, LANES), jnp.float32)
    return pl.pallas_call(
        functools.partial(project_kernel, plan, halves),
        out_shape=(low,),
        in_specs=[pl.BlockSpec(memory_space=pl.ANY)] * 8,
        out_specs=(pl.BlockSpec(memory_space=pltpu.VMEM),),
        scratch_shapes=[pltpu.VMEM(x.shape, x.dtype) for x in xs]
        + [pltpu.VMEM(w.shape, w.dtype) for w in ws]
        + [pltpu.SemaphoreType.DMA((len(plan),))] * 2,
        compiler_params=pltpu.CompilerParams(vmem_limit_bytes=VMEM_BYTES),
        name="project",
    )(*xs, *ws)


def stage_kernel(low_ref, out_ref):
    out_ref[...] = low_ref[...]


def stage(low):
    return pl.pallas_call(
        stage_kernel,
        out_shape=jax.ShapeDtypeStruct(low.shape, low.dtype),
        in_specs=[pl.BlockSpec(memory_space=pltpu.VMEM)],
        out_specs=pl.BlockSpec(memory_space=pltpu.VMEM),
        compiler_params=pltpu.CompilerParams(vmem_limit_bytes=SMALL_BYTES),
        name="stage",
    )(low)


def vectors_kernel(n_parts, n_sends, *refs):
    parts, seg_ref, wanted_ref, vec_ref = refs[:n_parts], *refs[n_parts : n_parts + 3]
    send_refs, slabs = refs[n_parts + 3 : n_parts + 3 + n_sends], refs[n_parts + 3 + n_sends]
    halves, rank = parts[0].shape[0], parts[0].shape[1] // 4
    fold = LANES // rank
    n_slabs = rank // fold
    col_slabs = vec_ref.shape[2] // LANES
    seg = seg_ref[...]
    lane = lax.broadcasted_iota(jnp.int32, (EX_DEV * n_slabs, LANES), 1)
    scale = (EX_DEV / TOK_DEV) ** 0.5

    def total(index):
        sums = [functools.reduce(lambda a, b: a + b, [part[h, index, :] for part in parts]) for h in range(halves)]
        return jnp.concatenate(sums, axis=1)

    for p in range(2):
        in_high, in_low = split(total(pl.ds(2 * p * rank, rank)))
        in_wide = jnp.concatenate([in_high, in_low, in_high], axis=1)
        in_wide = jnp.concatenate([in_wide] * fold, axis=0)
        rows = []
        for b in range(fold):
            out_rows = total(pl.ds((2 * p + 1) * rank + b, n_slabs, stride=fold))
            rows += [jnp.where(seg == e, out_rows, 0.0) for e in range(EX_DEV)]
        out_high, out_low = split(jnp.concatenate(rows, axis=0))
        out_wide = jnp.concatenate([out_high, out_high, out_low], axis=1)
        outer = lax.dot_general(out_wide, in_wide, NT, preferred_element_type=jnp.float32)
        flat = outer[: EX_DEV * n_slabs]
        for b in range(1, fold):
            block = outer[b * EX_DEV * n_slabs : (b + 1) * EX_DEV * n_slabs]
            flat = jnp.where(lane // rank == b, block, flat)
        flat = flat * scale
        for g in range(n_slabs):
            slabs[p * n_slabs + g] = jnp.concatenate(
                [flat[e * n_slabs + g : e * n_slabs + g + 1] for e in range(EX_DEV)], axis=0
            )
    t = lax.axis_index("tensor")
    columns = [[slabs[p * n_slabs + t * col_slabs + k] for k in range(col_slabs)] for p in range(2)]
    for p in range(2):
        for k in range(col_slabs):
            vec_ref[p, :, pl.ds(k * LANES, LANES)] = columns[p][k]
    rows = [slabs[s] for s in range(2 * n_slabs)]
    for j in range(wanted_ref.shape[0]):
        wanted = wanted_ref[j]
        row_slab = rows[0]
        for s in range(1, 2 * n_slabs):
            row_slab = jnp.where(wanted == s, rows[s], row_slab)
        if n_sends > 1:
            refs[-1][j] = row_slab
            continue
        send_refs[0][j, 0] = row_slab
        for k in range(col_slabs):
            send_refs[0][j, 1 + k] = jnp.where(wanted < n_slabs, columns[0][k], columns[1][k])
    if n_sends > 1:
        plane = lax.axis_index("dp") // PLANE
        for shift, send_ref in enumerate(send_refs):
            for p in range(2):
                for k in range(col_slabs):
                    send_ref[p * col_slabs + k] = columns[p][k]
            for d in range(PLANE):
                send_ref[2 * col_slabs + d] = refs[-1][lax.rem(plane + shift, n_sends) * PLANE + d]


def vectors(parts, segments, wanted, col_width, sends):
    n_slabs = (parts[0].shape[1] // 4) ** 2 // LANES
    vmem = pl.BlockSpec(memory_space=pltpu.VMEM)
    return pl.pallas_call(
        functools.partial(vectors_kernel, len(parts), len(sends)),
        out_shape=[jax.ShapeDtypeStruct((2, EX_DEV, col_width), jnp.float32)]
        + [jax.ShapeDtypeStruct(shape + (EX_DEV, LANES), jnp.float32) for shape in sends],
        in_specs=[vmem] * (len(parts) + 2),
        out_specs=[vmem] * (1 + len(sends)),
        scratch_shapes=[
            pltpu.VMEM((2 * n_slabs, EX_DEV, LANES), jnp.float32),
            pltpu.VMEM((wanted.shape[0], EX_DEV, LANES), jnp.float32),
        ],
        compiler_params=pltpu.CompilerParams(vmem_limit_bytes=SMALL_BYTES),
        name="vectors",
    )(*parts, segments, wanted)


def regroup_kernel(n_slabs, *refs):
    blocks, wanted_ref, outs = refs[: len(refs) // 2], refs[len(refs) // 2], refs[len(refs) // 2 + 1 :]
    col_slabs = (blocks[0].shape[0] - PLANE) // 2
    me = lax.axis_index("dp")
    plane, place = me // PLANE, lax.rem(me, PLANE)
    for step, out in zip((0,) + PLANE_STEPS, outs):
        target = place ^ step
        first = wanted_ref[plane * PLANE + target] < n_slabs
        for i, block in enumerate(blocks):
            rows = pl.ds(i * EX_DEV, EX_DEV)
            out[0, rows, :] = block[2 * col_slabs + target]
            for k in range(col_slabs):
                out[1 + k, rows, :] = jnp.where(first, block[k], block[col_slabs + k])


def regroup(blocks, wanted, n_slabs):
    col_slabs = (blocks[0].shape[0] - PLANE) // 2
    vmem = pl.BlockSpec(memory_space=pltpu.VMEM)
    part = jax.ShapeDtypeStruct((1 + col_slabs, len(blocks) * EX_DEV, LANES), jnp.float32)
    return pl.pallas_call(
        functools.partial(regroup_kernel, n_slabs),
        out_shape=[part] * PLANE,
        in_specs=[vmem] * (len(blocks) + 1),
        out_specs=[vmem] * PLANE,
        compiler_params=pltpu.CompilerParams(vmem_limit_bytes=SMALL_BYTES),
        name="regroup",
    )(*blocks, wanted)


def fisher_kernel(scale, n_parts, *refs):
    parts, vec_ref, (out_ref, vec_out, stack, full, sems) = refs[:n_parts], refs[n_parts], refs[-5:]
    store = pltpu.make_async_copy(vec_ref, vec_out, sems.at[0])
    store.start()
    examples, slabs = stack.shape[0], stack.shape[1] // LANES
    pieces = [part.at[i] for part in parts for i in range(part.shape[0])]
    rows = examples // len(pieces)
    for i, piece in enumerate(pieces):
        for k in range(slabs):
            stack[pl.ds(i * rows, rows), pl.ds(k * LANES, LANES)] = piece[k]
    own_rows, col_width = out_ref.shape[1:]
    start = 0
    if own_rows < LANES:
        start = (refs[n_parts + 1][lax.axis_index("dp")] * own_rows) % LANES
        start = pl.multiple_of(start, own_rows)
    row_high, row_low = split(stack[:, pl.ds(0, LANES)])
    row_wide = jnp.concatenate([row_high, row_high, row_low], axis=0)
    pieces = 2 if col_width % (2 * LANES) == 0 else 1
    size = col_width // pieces
    stores = [store]
    for c in range(pieces):
        col_high, col_low = split(stack[:, pl.ds(LANES + c * size, size)])
        col_wide = jnp.concatenate([col_high, col_low, col_high], axis=0)
        product = lax.dot_general(row_wide, col_wide, TN, preferred_element_type=jnp.float32)
        full[:, pl.ds(c * size, size)] = product * scale
        stores.append(
            pltpu.make_async_copy(
                full.at[pl.ds(start, own_rows), pl.ds(c * size, size)],
                out_ref.at[0, :, pl.ds(c * size, size)],
                sems.at[1 + c],
            )
        )
        stores[-1].start()
    for store in stores:
        store.wait()


def fisher(parts, vec, owner_map, own_rows):
    slabs = parts[0].shape[1]
    examples = sum(part.shape[0] * part.shape[2] for part in parts)
    col_width = (slabs - 1) * LANES
    hbm = pl.BlockSpec(memory_space=pl.ANY)
    owners = (owner_map,) if own_rows < LANES else ()
    return pl.pallas_call(
        functools.partial(fisher_kernel, 1.0 / examples, len(parts)),
        out_shape=(
            jax.ShapeDtypeStruct((1, own_rows, col_width), jnp.float32),
            jax.ShapeDtypeStruct(vec.shape, vec.dtype),
        ),
        in_specs=[pl.BlockSpec(memory_space=pltpu.VMEM)] * len(parts) + [hbm]
        + [pl.BlockSpec(memory_space=pltpu.SMEM)] * len(owners),
        out_specs=(hbm, hbm),
        scratch_shapes=[
            pltpu.VMEM((examples, slabs * LANES), jnp.float32),
            pltpu.VMEM((LANES, col_width), jnp.float32),
            pltpu.SemaphoreType.DMA((3,)),
        ],
        compiler_params=pltpu.CompilerParams(vmem_limit_bytes=SMALL_BYTES),
        name="fisher",
    )(*parts, vec, *owners)


def shards(
    o_inputs,
    o_gradients,
    up_inputs,
    up_gradients,
    o_in_proj,
    o_out_proj,
    up_in_proj,
    up_out_proj,
    segment_ids,
    owner_map,
):
    tensor_count = lax.axis_size("tensor")
    dp_count = lax.axis_size("dp")
    width = o_in_proj.shape[1] * o_out_proj.shape[1]
    col_width = width // tensor_count
    own_rows = 2 * width // dp_count
    (own,) = project(
        (o_inputs, o_gradients, up_inputs, up_gradients),
        (o_in_proj.T, o_out_proj.T, up_in_proj.T, up_out_proj.T),
    )
    if tensor_count == 2:
        parts = (stage(own), lax.ppermute(own, "tensor", [(0, 1), (1, 0)]))
    else:
        parts = (lax.psum(own, "tensor"),)
    wanted = jnp.broadcast_to((owner_map * own_rows // LANES)[:, None, None], (dp_count, EX_DEV, LANES))
    col_slabs = col_width // LANES
    planes = dp_count // PLANE
    if planes == 4 and own_rows == LANES:
        block = (2 * col_slabs + PLANE,)
        vec, *blocks = vectors(parts, segment_ids, wanted, col_width, [block] * planes)
        for shift in PLANE_SHIFTS:
            pairs = [(i, (i + shift * PLANE) % dp_count) for i in range(dp_count)]
            blocks[shift] = lax.ppermute(blocks[shift], "dp", pairs)
        grouped = regroup(blocks, wanted, width // LANES)
        recv = [grouped[0]]
        for part, step in zip(grouped[1:], PLANE_STEPS):
            recv.append(lax.ppermute(part, "dp", [(i, i ^ step) for i in range(dp_count)]))
        recv = [part[None] for part in recv]
    else:
        vec, send = vectors(parts, segment_ids, wanted, col_width, [(dp_count, 1 + col_slabs)])
        recv = [lax.all_to_all(send, "dp", 0, 0, tiled=True)]
    fisher_block, example_vectors = fisher(recv, vec, owner_map, own_rows)
    return example_vectors, fisher_block


def solution(mesh):
    in_specs = (
        P("dp", "tensor"),
        P("dp", "tensor"),
        P("dp", "tensor"),
        P("dp", "tensor"),
        P("tensor", None),
        P("tensor", None),
        P("tensor", None),
        P("tensor", None),
        P("dp", None),
        P(),
    )
    out_specs = (P(None, "dp", "tensor"), P("dp", None, "tensor"))
    return jax.shard_map(shards, mesh=mesh, in_specs=in_specs, out_specs=out_specs, check_vma=False)
```

```python
import functools

import jax
import jax.numpy as jnp
from jax import lax
from jax.experimental import pallas as pl
from jax.experimental.pallas import tpu as pltpu
from jax.sharding import PartitionSpec as P

TOK_DEV = 256
EX_DEV = 4
LANES = 128
NT = (((1,), (1,)), ((), ()))
TN = (((0,), (0,)), ((), ()))
PIECE = 4096
FIRST = (0, 3, 2, 1)
SECOND = (0, 8, 12, 4)
VMEM_BYTES = 54976 * 2**10
SMALL_BYTES = 8 * 2**20


def chunk_plan(widths):
    plan = []
    for which in sorted(range(len(widths)), key=lambda i: -widths[i]):
        start = 0
        while start < widths[which]:
            size = (widths[which] - start) % PIECE or PIECE
            plan.append((which, start, size))
            start += size
    return plan


def split(x):
    high = x.astype(jnp.bfloat16)
    return high, (x - high.astype(jnp.float32)).astype(jnp.bfloat16)


def project_kernel(plan, halves, *refs):
    x_hbm, w_hbm, outs = refs[0:4], refs[4:8], refs[8:9]
    x_vmem, w_vmem, x_sem, w_sem = refs[9:13], refs[13:17], refs[17], refs[18]
    w_copies, x_copies = [], []
    for n, (i, start, size) in enumerate(plan):
        piece = (slice(None), pl.ds(start, size))
        w_copies.append(pltpu.make_async_copy(w_hbm[i].at[piece], w_vmem[i].at[piece], w_sem.at[n]))
        x_copies.append(pltpu.make_async_copy(x_hbm[i].at[piece], x_vmem[i].at[piece], x_sem.at[n]))
        w_copies[n].start()
        x_copies[n].start()
    tokens, rank = x_vmem[0].shape[0], w_vmem[0].shape[0]
    part = tokens // halves
    totals = {}
    for n, (i, start, size) in enumerate(plan):
        w_copies[n].wait()
        x_copies[n].wait()
        w = w_vmem[i][:, pl.ds(start, size)]
        for h in range(halves):
            x = x_vmem[i][pl.ds(h * part, part), pl.ds(start, size)]
            product = lax.dot_general(x, w, NT, preferred_element_type=jnp.float32)
            totals[i, h] = product if start == 0 else totals[i, h] + product
    for i in range(4):
        for h in range(halves):
            low = totals[i, h].T
            for out in outs:
                out[h, pl.ds(i * rank, rank), :] = low


def project(xs, ws):
    plan = chunk_plan([x.shape[1] for x in xs])
    tokens, rank = xs[0].shape[0], ws[0].shape[0]
    halves = tokens // LANES
    low = jax.ShapeDtypeStruct((halves, 4 * rank, LANES), jnp.float32)
    return pl.pallas_call(
        functools.partial(project_kernel, plan, halves),
        out_shape=(low,),
        in_specs=[pl.BlockSpec(memory_space=pl.ANY)] * 8,
        out_specs=(pl.BlockSpec(memory_space=pltpu.VMEM),),
        scratch_shapes=[pltpu.VMEM(x.shape, x.dtype) for x in xs]
        + [pltpu.VMEM(w.shape, w.dtype) for w in ws]
        + [pltpu.SemaphoreType.DMA((len(plan),))] * 2,
        compiler_params=pltpu.CompilerParams(vmem_limit_bytes=VMEM_BYTES),
        name="project",
    )(*xs, *ws)


def stage_kernel(low_ref, out_ref):
    out_ref[...] = low_ref[...]


def stage(low):
    return pl.pallas_call(
        stage_kernel,
        out_shape=jax.ShapeDtypeStruct(low.shape, low.dtype),
        in_specs=[pl.BlockSpec(memory_space=pltpu.VMEM)],
        out_specs=pl.BlockSpec(memory_space=pltpu.VMEM),
        compiler_params=pltpu.CompilerParams(vmem_limit_bytes=SMALL_BYTES),
        name="stage",
    )(low)


def vectors_kernel(n_parts, n_sends, *refs):
    parts, seg_ref, wanted_ref, vec_ref = refs[:n_parts], *refs[n_parts : n_parts + 3]
    send_refs, slabs = refs[n_parts + 3 : n_parts + 3 + n_sends], refs[n_parts + 3 + n_sends]
    halves, rank = parts[0].shape[0], parts[0].shape[1] // 4
    fold = LANES // rank
    n_slabs = rank // fold
    col_slabs = vec_ref.shape[2] // LANES
    seg = seg_ref[...]
    lane = lax.broadcasted_iota(jnp.int32, (EX_DEV * n_slabs, LANES), 1)
    scale = (EX_DEV / TOK_DEV) ** 0.5

    def total(index):
        sums = [functools.reduce(lambda a, b: a + b, [part[h, index, :] for part in parts]) for h in range(halves)]
        return jnp.concatenate(sums, axis=1)

    for p in range(2):
        in_high, in_low = split(total(pl.ds(2 * p * rank, rank)))
        in_wide = jnp.concatenate([in_high, in_low, in_high], axis=1)
        in_wide = jnp.concatenate([in_wide] * fold, axis=0)
        rows = []
        for b in range(fold):
            out_rows = total(pl.ds((2 * p + 1) * rank + b, n_slabs, stride=fold))
            rows += [jnp.where(seg == e, out_rows, 0.0) for e in range(EX_DEV)]
        out_high, out_low = split(jnp.concatenate(rows, axis=0))
        out_wide = jnp.concatenate([out_high, out_high, out_low], axis=1)
        outer = lax.dot_general(out_wide, in_wide, NT, preferred_element_type=jnp.float32)
        flat = outer[: EX_DEV * n_slabs]
        for b in range(1, fold):
            block = outer[b * EX_DEV * n_slabs : (b + 1) * EX_DEV * n_slabs]
            flat = jnp.where(lane // rank == b, block, flat)
        flat = flat * scale
        for g in range(n_slabs):
            slabs[p * n_slabs + g] = jnp.concatenate(
                [flat[e * n_slabs + g : e * n_slabs + g + 1] for e in range(EX_DEV)], axis=0
            )
    t = lax.axis_index("tensor")
    columns = [[slabs[p * n_slabs + t * col_slabs + k] for k in range(col_slabs)] for p in range(2)]
    for p in range(2):
        for k in range(col_slabs):
            vec_ref[p, :, pl.ds(k * LANES, LANES)] = columns[p][k]
    rows = [slabs[s] for s in range(2 * n_slabs)]
    for j in range(wanted_ref.shape[0]):
        wanted = wanted_ref[j]
        row_slab = rows[0]
        for s in range(1, 2 * n_slabs):
            row_slab = jnp.where(wanted == s, rows[s], row_slab)
        if n_sends > 1:
            refs[-1][j] = row_slab
            continue
        send_refs[0][j, 0] = row_slab
        for k in range(col_slabs):
            send_refs[0][j, 1 + k] = jnp.where(wanted < n_slabs, columns[0][k], columns[1][k])
    if n_sends > 1:
        me = lax.axis_index("dp")
        for target, send_ref in zip(FIRST, send_refs):
            for p in range(2):
                for k in range(col_slabs):
                    send_ref[p * col_slabs + k] = columns[p][k]
            for d, step in enumerate(SECOND):
                send_ref[2 * col_slabs + d] = refs[-1][me ^ target ^ step]


def vectors(parts, segments, wanted, col_width, sends):
    n_slabs = (parts[0].shape[1] // 4) ** 2 // LANES
    vmem = pl.BlockSpec(memory_space=pltpu.VMEM)
    return pl.pallas_call(
        functools.partial(vectors_kernel, len(parts), len(sends)),
        out_shape=[jax.ShapeDtypeStruct((2, EX_DEV, col_width), jnp.float32)]
        + [jax.ShapeDtypeStruct(shape + (EX_DEV, LANES), jnp.float32) for shape in sends],
        in_specs=[vmem] * (len(parts) + 2),
        out_specs=[vmem] * (1 + len(sends)),
        scratch_shapes=[
            pltpu.VMEM((2 * n_slabs, EX_DEV, LANES), jnp.float32),
            pltpu.VMEM((wanted.shape[0], EX_DEV, LANES), jnp.float32),
        ],
        compiler_params=pltpu.CompilerParams(vmem_limit_bytes=SMALL_BYTES),
        name="vectors",
    )(*parts, segments, wanted)


def regroup_kernel(n_slabs, *refs):
    blocks, wanted_ref, outs = refs[: len(FIRST)], refs[len(FIRST)], refs[len(FIRST) + 1 :]
    col_slabs = (blocks[0].shape[0] - len(SECOND)) // 2
    me = lax.axis_index("dp")
    for d, (step, out) in enumerate(zip(SECOND, outs)):
        first = wanted_ref[me ^ step] < n_slabs
        for i, block in enumerate(blocks):
            rows = pl.ds(i * EX_DEV, EX_DEV)
            out[0, rows, :] = block[2 * col_slabs + d]
            for k in range(col_slabs):
                out[1 + k, rows, :] = jnp.where(first, block[k], block[col_slabs + k])


def regroup(blocks, wanted, n_slabs):
    col_slabs = (blocks[0].shape[0] - len(SECOND)) // 2
    vmem = pl.BlockSpec(memory_space=pltpu.VMEM)
    part = jax.ShapeDtypeStruct((1 + col_slabs, len(blocks) * EX_DEV, LANES), jnp.float32)
    return pl.pallas_call(
        functools.partial(regroup_kernel, n_slabs),
        out_shape=[part] * len(SECOND),
        in_specs=[vmem] * (len(blocks) + 1),
        out_specs=[vmem] * len(SECOND),
        compiler_params=pltpu.CompilerParams(vmem_limit_bytes=SMALL_BYTES),
        name="regroup",
    )(*blocks, wanted)


def fisher_kernel(scale, n_parts, *refs):
    parts, vec_ref, (out_ref, vec_out, stack, full, sems) = refs[:n_parts], refs[n_parts], refs[-5:]
    store = pltpu.make_async_copy(vec_ref, vec_out, sems.at[0])
    store.start()
    examples, slabs = stack.shape[0], stack.shape[1] // LANES
    pieces = [part.at[i] for part in parts for i in range(part.shape[0])]
    rows = examples // len(pieces)
    for i, piece in enumerate(pieces):
        for k in range(slabs):
            stack[pl.ds(i * rows, rows), pl.ds(k * LANES, LANES)] = piece[k]
    own_rows, col_width = out_ref.shape[1:]
    start = 0
    if own_rows < LANES:
        start = (refs[n_parts + 1][lax.axis_index("dp")] * own_rows) % LANES
        start = pl.multiple_of(start, own_rows)
    row_high, row_low = split(stack[:, pl.ds(0, LANES)])
    row_wide = jnp.concatenate([row_high, row_high, row_low], axis=0)
    pieces = 2 if col_width % (2 * LANES) == 0 else 1
    size = col_width // pieces
    stores = [store]
    for c in range(pieces):
        col_high, col_low = split(stack[:, pl.ds(LANES + c * size, size)])
        col_wide = jnp.concatenate([col_high, col_low, col_high], axis=0)
        product = lax.dot_general(row_wide, col_wide, TN, preferred_element_type=jnp.float32)
        full[:, pl.ds(c * size, size)] = product * scale
        stores.append(
            pltpu.make_async_copy(
                full.at[pl.ds(start, own_rows), pl.ds(c * size, size)],
                out_ref.at[0, :, pl.ds(c * size, size)],
                sems.at[1 + c],
            )
        )
        stores[-1].start()
    for store in stores:
        store.wait()


def fisher(parts, vec, owner_map, own_rows):
    slabs = parts[0].shape[1]
    examples = sum(part.shape[0] * part.shape[2] for part in parts)
    col_width = (slabs - 1) * LANES
    hbm = pl.BlockSpec(memory_space=pl.ANY)
    owners = (owner_map,) if own_rows < LANES else ()
    return pl.pallas_call(
        functools.partial(fisher_kernel, 1.0 / examples, len(parts)),
        out_shape=(
            jax.ShapeDtypeStruct((1, own_rows, col_width), jnp.float32),
            jax.ShapeDtypeStruct(vec.shape, vec.dtype),
        ),
        in_specs=[pl.BlockSpec(memory_space=pltpu.VMEM)] * len(parts) + [hbm]
        + [pl.BlockSpec(memory_space=pltpu.SMEM)] * len(owners),
        out_specs=(hbm, hbm),
        scratch_shapes=[
            pltpu.VMEM((examples, slabs * LANES), jnp.float32),
            pltpu.VMEM((LANES, col_width), jnp.float32),
            pltpu.SemaphoreType.DMA((3,)),
        ],
        compiler_params=pltpu.CompilerParams(vmem_limit_bytes=SMALL_BYTES),
        name="fisher",
    )(*parts, vec, *owners)


def shards(
    o_inputs,
    o_gradients,
    up_inputs,
    up_gradients,
    o_in_proj,
    o_out_proj,
    up_in_proj,
    up_out_proj,
    segment_ids,
    owner_map,
):
    tensor_count = lax.axis_size("tensor")
    dp_count = lax.axis_size("dp")
    width = o_in_proj.shape[1] * o_out_proj.shape[1]
    col_width = width // tensor_count
    own_rows = 2 * width // dp_count
    (own,) = project(
        (o_inputs, o_gradients, up_inputs, up_gradients),
        (o_in_proj.T, o_out_proj.T, up_in_proj.T, up_out_proj.T),
    )
    if tensor_count == 2:
        parts = (stage(own), lax.ppermute(own, "tensor", [(0, 1), (1, 0)]))
    else:
        parts = (lax.psum(own, "tensor"),)
    wanted = jnp.broadcast_to((owner_map * own_rows // LANES)[:, None, None], (dp_count, EX_DEV, LANES))
    col_slabs = col_width // LANES
    if dp_count == len(FIRST) * len(SECOND) and own_rows == LANES:
        block = (2 * col_slabs + len(SECOND),)
        vec, *blocks = vectors(parts, segment_ids, wanted, col_width, [block] * len(FIRST))
        for n, step in enumerate(FIRST[1:], 1):
            blocks[n] = lax.ppermute(blocks[n], "dp", [(i, i ^ step) for i in range(dp_count)])
        recv = list(regroup(blocks, wanted, width // LANES))
        for n, step in enumerate(SECOND[1:], 1):
            recv[n] = lax.ppermute(recv[n], "dp", [(i, i ^ step) for i in range(dp_count)])
        recv = [part[None] for part in recv]
    else:
        vec, send = vectors(parts, segment_ids, wanted, col_width, [(dp_count, 1 + col_slabs)])
        recv = [lax.all_to_all(send, "dp", 0, 0, tiled=True)]
    fisher_block, example_vectors = fisher(recv, vec, owner_map, own_rows)
    return example_vectors, fisher_block


def solution(mesh):
    in_specs = (
        P("dp", "tensor"),
        P("dp", "tensor"),
        P("dp", "tensor"),
        P("dp", "tensor"),
        P("tensor", None),
        P("tensor", None),
        P("tensor", None),
        P("tensor", None),
        P("dp", None),
        P(),
    )
    out_specs = (P(None, "dp", "tensor"), P("dp", None, "tensor"))
    return jax.shard_map(shards, mesh=mesh, in_specs=in_specs, out_specs=out_specs, check_vma=False)
```

```python
import functools

import jax
import jax.numpy as jnp
from jax import lax
from jax.experimental import pallas as pl
from jax.experimental.pallas import tpu as pltpu
from jax.sharding import PartitionSpec as P

TOK_DEV = 256
EX_DEV = 4
LANES = 128
NT = (((1,), (1,)), ((), ()))
TN = (((0,), (0,)), ((), ()))
PIECE = 4096
FIRST = (0, 3, 2, 1)
SECOND = (0, 4, 8, 12)
LAST = len(FIRST) * len(SECOND) - 1
VMEM_BYTES = 54976 * 2**10
SMALL_BYTES = 8 * 2**20


def chunk_plan(widths):
    plan = []
    for which in sorted(range(len(widths)), key=lambda i: -widths[i]):
        start = 0
        while start < widths[which]:
            size = (widths[which] - start) % PIECE or PIECE
            plan.append((which, start, size))
            start += size
    return plan


def split(x):
    high = x.astype(jnp.bfloat16)
    return high, (x - high.astype(jnp.float32)).astype(jnp.bfloat16)


def project_kernel(plan, halves, *refs):
    x_hbm, w_hbm, outs = refs[0:4], refs[4:8], refs[8:9]
    x_vmem, w_vmem, x_sem, w_sem = refs[9:13], refs[13:17], refs[17], refs[18]
    w_copies, x_copies = [], []
    for n, (i, start, size) in enumerate(plan):
        piece = (slice(None), pl.ds(start, size))
        w_copies.append(pltpu.make_async_copy(w_hbm[i].at[piece], w_vmem[i].at[piece], w_sem.at[n]))
        x_copies.append(pltpu.make_async_copy(x_hbm[i].at[piece], x_vmem[i].at[piece], x_sem.at[n]))
        w_copies[n].start()
        x_copies[n].start()
    tokens, rank = x_vmem[0].shape[0], w_vmem[0].shape[0]
    part = tokens // halves
    totals = {}
    for n, (i, start, size) in enumerate(plan):
        w_copies[n].wait()
        x_copies[n].wait()
        w = w_vmem[i][:, pl.ds(start, size)]
        for h in range(halves):
            x = x_vmem[i][pl.ds(h * part, part), pl.ds(start, size)]
            product = lax.dot_general(x, w, NT, preferred_element_type=jnp.float32)
            totals[i, h] = product if start == 0 else totals[i, h] + product
    for i in range(4):
        for h in range(halves):
            low = totals[i, h].T
            for out in outs:
                out[h, pl.ds(i * rank, rank), :] = low


def project(xs, ws):
    plan = chunk_plan([x.shape[1] for x in xs])
    tokens, rank = xs[0].shape[0], ws[0].shape[0]
    halves = tokens // LANES
    low = jax.ShapeDtypeStruct((halves, 4 * rank, LANES), jnp.float32)
    return pl.pallas_call(
        functools.partial(project_kernel, plan, halves),
        out_shape=(low,),
        in_specs=[pl.BlockSpec(memory_space=pl.ANY)] * 8,
        out_specs=(pl.BlockSpec(memory_space=pltpu.VMEM),),
        scratch_shapes=[pltpu.VMEM(x.shape, x.dtype) for x in xs]
        + [pltpu.VMEM(w.shape, w.dtype) for w in ws]
        + [pltpu.SemaphoreType.DMA((len(plan),))] * 2,
        compiler_params=pltpu.CompilerParams(vmem_limit_bytes=VMEM_BYTES),
        name="project",
    )(*xs, *ws)


def stage_kernel(low_ref, out_ref):
    out_ref[...] = low_ref[...]


def stage(low):
    return pl.pallas_call(
        stage_kernel,
        out_shape=jax.ShapeDtypeStruct(low.shape, low.dtype),
        in_specs=[pl.BlockSpec(memory_space=pltpu.VMEM)],
        out_specs=pl.BlockSpec(memory_space=pltpu.VMEM),
        compiler_params=pltpu.CompilerParams(vmem_limit_bytes=SMALL_BYTES),
        name="stage",
    )(low)


def vectors_kernel(n_parts, n_sends, *refs):
    parts, seg_ref, wanted_ref, vec_ref = refs[:n_parts], *refs[n_parts : n_parts + 3]
    send_refs, slabs = refs[n_parts + 3 : n_parts + 3 + n_sends], refs[n_parts + 3 + n_sends]
    halves, rank = parts[0].shape[0], parts[0].shape[1] // 4
    fold = LANES // rank
    n_slabs = rank // fold
    col_slabs = vec_ref.shape[2] // LANES
    seg = seg_ref[...]
    lane = lax.broadcasted_iota(jnp.int32, (EX_DEV * n_slabs, LANES), 1)
    scale = (EX_DEV / TOK_DEV) ** 0.5

    def total(index):
        sums = [functools.reduce(lambda a, b: a + b, [part[h, index, :] for part in parts]) for h in range(halves)]
        return jnp.concatenate(sums, axis=1)

    for p in range(2):
        in_high, in_low = split(total(pl.ds(2 * p * rank, rank)))
        in_wide = jnp.concatenate([in_high, in_low, in_high], axis=1)
        in_wide = jnp.concatenate([in_wide] * fold, axis=0)
        rows = []
        for b in range(fold):
            out_rows = total(pl.ds((2 * p + 1) * rank + b, n_slabs, stride=fold))
            rows += [jnp.where(seg == e, out_rows, 0.0) for e in range(EX_DEV)]
        out_high, out_low = split(jnp.concatenate(rows, axis=0))
        out_wide = jnp.concatenate([out_high, out_high, out_low], axis=1)
        outer = lax.dot_general(out_wide, in_wide, NT, preferred_element_type=jnp.float32)
        flat = outer[: EX_DEV * n_slabs]
        for b in range(1, fold):
            block = outer[b * EX_DEV * n_slabs : (b + 1) * EX_DEV * n_slabs]
            flat = jnp.where(lane // rank == b, block, flat)
        flat = flat * scale
        for g in range(n_slabs):
            slabs[p * n_slabs + g] = jnp.concatenate(
                [flat[e * n_slabs + g : e * n_slabs + g + 1] for e in range(EX_DEV)], axis=0
            )
    t = lax.axis_index("tensor")
    columns = [[slabs[p * n_slabs + t * col_slabs + k] for k in range(col_slabs)] for p in range(2)]
    for p in range(2):
        for k in range(col_slabs):
            vec_ref[p, :, pl.ds(k * LANES, LANES)] = columns[p][k]
    rows = [slabs[s] for s in range(2 * n_slabs)]
    for j in range(wanted_ref.shape[0]):
        wanted = wanted_ref[j]
        row_slab = rows[0]
        for s in range(1, 2 * n_slabs):
            row_slab = jnp.where(wanted == s, rows[s], row_slab)
        if n_sends > 1:
            refs[-1][j] = row_slab
            continue
        send_refs[0][j, 0] = row_slab
        for k in range(col_slabs):
            send_refs[0][j, 1 + k] = jnp.where(wanted < n_slabs, columns[0][k], columns[1][k])
    if n_sends > 1:
        me = lax.axis_index("dp")
        for target, send_ref in zip(FIRST, send_refs):
            for p in range(2):
                for k in range(col_slabs):
                    send_ref[p * col_slabs + k] = columns[p][k]
            for d, step in enumerate(SECOND):
                send_ref[2 * col_slabs + d] = refs[-1][((me ^ target) + step) & LAST]


def vectors(parts, segments, wanted, col_width, sends):
    n_slabs = (parts[0].shape[1] // 4) ** 2 // LANES
    vmem = pl.BlockSpec(memory_space=pltpu.VMEM)
    return pl.pallas_call(
        functools.partial(vectors_kernel, len(parts), len(sends)),
        out_shape=[jax.ShapeDtypeStruct((2, EX_DEV, col_width), jnp.float32)]
        + [jax.ShapeDtypeStruct(shape + (EX_DEV, LANES), jnp.float32) for shape in sends],
        in_specs=[vmem] * (len(parts) + 2),
        out_specs=[vmem] * (1 + len(sends)),
        scratch_shapes=[
            pltpu.VMEM((2 * n_slabs, EX_DEV, LANES), jnp.float32),
            pltpu.VMEM((wanted.shape[0], EX_DEV, LANES), jnp.float32),
        ],
        compiler_params=pltpu.CompilerParams(vmem_limit_bytes=SMALL_BYTES),
        name="vectors",
    )(*parts, segments, wanted)


def regroup_kernel(n_slabs, *refs):
    blocks, wanted_ref, outs = refs[: len(FIRST)], refs[len(FIRST)], refs[len(FIRST) + 1 :]
    col_slabs = (blocks[0].shape[0] - len(SECOND)) // 2
    me = lax.axis_index("dp")
    for d, (step, out) in enumerate(zip(SECOND, outs)):
        first = wanted_ref[(me + step) & LAST] < n_slabs
        for i, block in enumerate(blocks):
            rows = pl.ds(i * EX_DEV, EX_DEV)
            out[0, rows, :] = block[2 * col_slabs + d]
            for k in range(col_slabs):
                out[1 + k, rows, :] = jnp.where(first, block[k], block[col_slabs + k])


def regroup(blocks, wanted, n_slabs):
    col_slabs = (blocks[0].shape[0] - len(SECOND)) // 2
    vmem = pl.BlockSpec(memory_space=pltpu.VMEM)
    part = jax.ShapeDtypeStruct((1 + col_slabs, len(blocks) * EX_DEV, LANES), jnp.float32)
    return pl.pallas_call(
        functools.partial(regroup_kernel, n_slabs),
        out_shape=[part] * len(SECOND),
        in_specs=[vmem] * (len(blocks) + 1),
        out_specs=[vmem] * len(SECOND),
        compiler_params=pltpu.CompilerParams(vmem_limit_bytes=SMALL_BYTES),
        name="regroup",
    )(*blocks, wanted)


def fisher_kernel(scale, n_parts, *refs):
    parts, vec_ref, (out_ref, vec_out, stack, full, sems) = refs[:n_parts], refs[n_parts], refs[-5:]
    store = pltpu.make_async_copy(vec_ref, vec_out, sems.at[0])
    store.start()
    examples, slabs = stack.shape[0], stack.shape[1] // LANES
    pieces = [part.at[i] for part in parts for i in range(part.shape[0])]
    rows = examples // len(pieces)
    for i, piece in enumerate(pieces):
        for k in range(slabs):
            stack[pl.ds(i * rows, rows), pl.ds(k * LANES, LANES)] = piece[k]
    own_rows, col_width = out_ref.shape[1:]
    start = 0
    if own_rows < LANES:
        start = (refs[n_parts + 1][lax.axis_index("dp")] * own_rows) % LANES
        start = pl.multiple_of(start, own_rows)
    row_high, row_low = split(stack[:, pl.ds(0, LANES)])
    row_wide = jnp.concatenate([row_high, row_high, row_low], axis=0)
    pieces = 2 if col_width % (2 * LANES) == 0 else 1
    size = col_width // pieces
    stores = [store]
    for c in range(pieces):
        col_high, col_low = split(stack[:, pl.ds(LANES + c * size, size)])
        col_wide = jnp.concatenate([col_high, col_low, col_high], axis=0)
        product = lax.dot_general(row_wide, col_wide, TN, preferred_element_type=jnp.float32)
        full[:, pl.ds(c * size, size)] = product * scale
        stores.append(
            pltpu.make_async_copy(
                full.at[pl.ds(start, own_rows), pl.ds(c * size, size)],
                out_ref.at[0, :, pl.ds(c * size, size)],
                sems.at[1 + c],
            )
        )
        stores[-1].start()
    for store in stores:
        store.wait()


def fisher(parts, vec, owner_map, own_rows):
    slabs = parts[0].shape[1]
    examples = sum(part.shape[0] * part.shape[2] for part in parts)
    col_width = (slabs - 1) * LANES
    hbm = pl.BlockSpec(memory_space=pl.ANY)
    owners = (owner_map,) if own_rows < LANES else ()
    return pl.pallas_call(
        functools.partial(fisher_kernel, 1.0 / examples, len(parts)),
        out_shape=(
            jax.ShapeDtypeStruct((1, own_rows, col_width), jnp.float32),
            jax.ShapeDtypeStruct(vec.shape, vec.dtype),
        ),
        in_specs=[pl.BlockSpec(memory_space=pltpu.VMEM)] * len(parts) + [hbm]
        + [pl.BlockSpec(memory_space=pltpu.SMEM)] * len(owners),
        out_specs=(hbm, hbm),
        scratch_shapes=[
            pltpu.VMEM((examples, slabs * LANES), jnp.float32),
            pltpu.VMEM((LANES, col_width), jnp.float32),
            pltpu.SemaphoreType.DMA((3,)),
        ],
        compiler_params=pltpu.CompilerParams(vmem_limit_bytes=SMALL_BYTES),
        name="fisher",
    )(*parts, vec, *owners)


def shards(
    o_inputs,
    o_gradients,
    up_inputs,
    up_gradients,
    o_in_proj,
    o_out_proj,
    up_in_proj,
    up_out_proj,
    segment_ids,
    owner_map,
):
    tensor_count = lax.axis_size("tensor")
    dp_count = lax.axis_size("dp")
    width = o_in_proj.shape[1] * o_out_proj.shape[1]
    col_width = width // tensor_count
    own_rows = 2 * width // dp_count
    (own,) = project(
        (o_inputs, o_gradients, up_inputs, up_gradients),
        (o_in_proj.T, o_out_proj.T, up_in_proj.T, up_out_proj.T),
    )
    if tensor_count == 2:
        parts = (stage(own), lax.ppermute(own, "tensor", [(0, 1), (1, 0)]))
    else:
        parts = (lax.psum(own, "tensor"),)
    wanted = jnp.broadcast_to((owner_map * own_rows // LANES)[:, None, None], (dp_count, EX_DEV, LANES))
    col_slabs = col_width // LANES
    if dp_count == len(FIRST) * len(SECOND) and own_rows == LANES:
        block = (2 * col_slabs + len(SECOND),)
        vec, *blocks = vectors(parts, segment_ids, wanted, col_width, [block] * len(FIRST))
        for n, step in enumerate(FIRST[1:], 1):
            blocks[n] = lax.ppermute(blocks[n], "dp", [(i, i ^ step) for i in range(dp_count)])
        recv = list(regroup(blocks, wanted, width // LANES))
        for n, step in enumerate(SECOND[1:], 1):
            recv[n] = lax.ppermute(recv[n], "dp", [(i, (i + step) & LAST) for i in range(dp_count)])
        recv = [part[None] for part in recv]
    else:
        vec, send = vectors(parts, segment_ids, wanted, col_width, [(dp_count, 1 + col_slabs)])
        recv = [lax.all_to_all(send, "dp", 0, 0, tiled=True)]
    fisher_block, example_vectors = fisher(recv, vec, owner_map, own_rows)
    return example_vectors, fisher_block


def solution(mesh):
    in_specs = (
        P("dp", "tensor"),
        P("dp", "tensor"),
        P("dp", "tensor"),
        P("dp", "tensor"),
        P("tensor", None),
        P("tensor", None),
        P("tensor", None),
        P("tensor", None),
        P("dp", None),
        P(),
    )
    out_specs = (P(None, "dp", "tensor"), P("dp", None, "tensor"))
    return jax.shard_map(shards, mesh=mesh, in_specs=in_specs, out_specs=out_specs, check_vma=False)
```

```python
import functools

import jax
import jax.numpy as jnp
from jax import lax
from jax.experimental import pallas as pl
from jax.experimental.pallas import tpu as pltpu
from jax.sharding import PartitionSpec as P

TOK_DEV = 256
EX_DEV = 4
LANES = 128
NT = (((1,), (1,)), ((), ()))
TN = (((0,), (0,)), ((), ()))
PIECE = 4096
FIRST = (0, 3, 2, 1)
SECOND = (0, 4, 8, 12)
LAST = len(FIRST) * len(SECOND) - 1
VMEM_BYTES = 54976 * 2**10
SMALL_BYTES = 8 * 2**20


def chunk_plan(widths):
    plan = []
    for which in sorted(range(len(widths)), key=lambda i: -widths[i]):
        start = 0
        while start < widths[which]:
            size = (widths[which] - start) % PIECE or PIECE
            plan.append((which, start, size))
            start += size
    return plan


def split(x):
    high = x.astype(jnp.bfloat16)
    return high, (x - high.astype(jnp.float32)).astype(jnp.bfloat16)


def project_kernel(plan, halves, *refs):
    x_hbm, w_hbm, outs = refs[0:4], refs[4:8], refs[8:9]
    x_vmem, w_vmem, x_sem, w_sem = refs[9:13], refs[13:17], refs[17], refs[18]
    w_copies, x_copies = [], []
    for n, (i, start, size) in enumerate(plan):
        piece = (slice(None), pl.ds(start, size))
        w_copies.append(pltpu.make_async_copy(w_hbm[i].at[piece], w_vmem[i].at[piece], w_sem.at[n]))
        x_copies.append(pltpu.make_async_copy(x_hbm[i].at[piece], x_vmem[i].at[piece], x_sem.at[n]))
        x_copies[n].start()
        w_copies[n].start()
    tokens, rank = x_vmem[0].shape[0], w_vmem[0].shape[0]
    part = tokens // halves
    totals = {}
    for n, (i, start, size) in enumerate(plan):
        w_copies[n].wait()
        x_copies[n].wait()
        w = w_vmem[i][:, pl.ds(start, size)]
        for h in range(halves):
            x = x_vmem[i][pl.ds(h * part, part), pl.ds(start, size)]
            product = lax.dot_general(x, w, NT, preferred_element_type=jnp.float32)
            totals[i, h] = product if start == 0 else totals[i, h] + product
    for i in range(4):
        for h in range(halves):
            low = totals[i, h].T
            for out in outs:
                out[h, pl.ds(i * rank, rank), :] = low


def project(xs, ws):
    plan = chunk_plan([x.shape[1] for x in xs])
    tokens, rank = xs[0].shape[0], ws[0].shape[0]
    halves = tokens // LANES
    low = jax.ShapeDtypeStruct((halves, 4 * rank, LANES), jnp.float32)
    return pl.pallas_call(
        functools.partial(project_kernel, plan, halves),
        out_shape=(low,),
        in_specs=[pl.BlockSpec(memory_space=pl.ANY)] * 8,
        out_specs=(pl.BlockSpec(memory_space=pltpu.VMEM),),
        scratch_shapes=[pltpu.VMEM(x.shape, x.dtype) for x in xs]
        + [pltpu.VMEM(w.shape, w.dtype) for w in ws]
        + [pltpu.SemaphoreType.DMA((len(plan),))] * 2,
        compiler_params=pltpu.CompilerParams(vmem_limit_bytes=VMEM_BYTES),
        name="project",
    )(*xs, *ws)


def stage_kernel(low_ref, wanted_ref, low_out, wanted_out):
    low_out[...] = low_ref[...]
    wanted_out[...] = wanted_ref[...]


def stage(low, wanted):
    vmem = pl.BlockSpec(memory_space=pltpu.VMEM)
    return pl.pallas_call(
        stage_kernel,
        out_shape=[jax.ShapeDtypeStruct(x.shape, x.dtype) for x in (low, wanted)],
        in_specs=[vmem] * 2,
        out_specs=[vmem] * 2,
        compiler_params=pltpu.CompilerParams(vmem_limit_bytes=SMALL_BYTES),
        name="stage",
    )(low, wanted)


def vectors_kernel(n_parts, n_sends, *refs):
    parts, seg_ref, wanted_ref, vec_ref = refs[:n_parts], *refs[n_parts : n_parts + 3]
    send_refs, slabs = refs[n_parts + 3 : n_parts + 3 + n_sends], refs[n_parts + 3 + n_sends]
    halves, rank = parts[0].shape[0], parts[0].shape[1] // 4
    fold = LANES // rank
    n_slabs = rank // fold
    col_slabs = vec_ref.shape[2] // LANES
    seg = seg_ref[...]
    lane = lax.broadcasted_iota(jnp.int32, (EX_DEV * n_slabs, LANES), 1)
    scale = (EX_DEV / TOK_DEV) ** 0.5

    def total(index):
        sums = [functools.reduce(lambda a, b: a + b, [part[h, index, :] for part in parts]) for h in range(halves)]
        return jnp.concatenate(sums, axis=1)

    for p in range(2):
        in_high, in_low = split(total(pl.ds(2 * p * rank, rank)))
        in_wide = jnp.concatenate([in_high, in_low, in_high], axis=1)
        in_wide = jnp.concatenate([in_wide] * fold, axis=0)
        rows = []
        for b in range(fold):
            out_rows = total(pl.ds((2 * p + 1) * rank + b, n_slabs, stride=fold))
            rows += [jnp.where(seg == e, out_rows, 0.0) for e in range(EX_DEV)]
        out_high, out_low = split(jnp.concatenate(rows, axis=0))
        out_wide = jnp.concatenate([out_high, out_high, out_low], axis=1)
        outer = lax.dot_general(out_wide, in_wide, NT, preferred_element_type=jnp.float32)
        flat = outer[: EX_DEV * n_slabs]
        for b in range(1, fold):
            block = outer[b * EX_DEV * n_slabs : (b + 1) * EX_DEV * n_slabs]
            flat = jnp.where(lane // rank == b, block, flat)
        flat = flat * scale
        for g in range(n_slabs):
            slabs[p * n_slabs + g] = jnp.concatenate(
                [flat[e * n_slabs + g : e * n_slabs + g + 1] for e in range(EX_DEV)], axis=0
            )
    t = lax.axis_index("tensor")
    columns = [[slabs[p * n_slabs + t * col_slabs + k] for k in range(col_slabs)] for p in range(2)]
    for p in range(2):
        for k in range(col_slabs):
            vec_ref[p, :, pl.ds(k * LANES, LANES)] = columns[p][k]
    rows = [slabs[s] for s in range(2 * n_slabs)]
    for j in range(wanted_ref.shape[0]):
        wanted = wanted_ref[j]
        row_slab = rows[0]
        for s in range(1, 2 * n_slabs):
            row_slab = jnp.where(wanted == s, rows[s], row_slab)
        if n_sends > 1:
            refs[-1][j] = row_slab
            continue
        send_refs[0][j, 0] = row_slab
        for k in range(col_slabs):
            send_refs[0][j, 1 + k] = jnp.where(wanted < n_slabs, columns[0][k], columns[1][k])
    if n_sends > 1:
        me = lax.axis_index("dp")
        for target, send_ref in zip(FIRST, send_refs):
            for p in range(2):
                for k in range(col_slabs):
                    send_ref[p * col_slabs + k] = columns[p][k]
            for d, step in enumerate(SECOND):
                send_ref[2 * col_slabs + d] = refs[-1][((me ^ target) + step) & LAST]


def vectors(parts, segments, wanted, col_width, sends):
    n_slabs = (parts[0].shape[1] // 4) ** 2 // LANES
    vmem = pl.BlockSpec(memory_space=pltpu.VMEM)
    return pl.pallas_call(
        functools.partial(vectors_kernel, len(parts), len(sends)),
        out_shape=[jax.ShapeDtypeStruct((2, EX_DEV, col_width), jnp.float32)]
        + [jax.ShapeDtypeStruct(shape + (EX_DEV, LANES), jnp.float32) for shape in sends],
        in_specs=[vmem] * (len(parts) + 2),
        out_specs=[vmem] * (1 + len(sends)),
        scratch_shapes=[
            pltpu.VMEM((2 * n_slabs, EX_DEV, LANES), jnp.float32),
            pltpu.VMEM((wanted.shape[0], EX_DEV, LANES), jnp.float32),
        ],
        compiler_params=pltpu.CompilerParams(vmem_limit_bytes=SMALL_BYTES),
        name="vectors",
    )(*parts, segments, wanted)


def regroup_kernel(n_slabs, *refs):
    blocks, wanted_ref, outs = refs[: len(FIRST)], refs[len(FIRST)], refs[len(FIRST) + 1 :]
    col_slabs = (blocks[0].shape[0] - len(SECOND)) // 2
    me = lax.axis_index("dp")
    for d, (step, out) in enumerate(zip(SECOND, outs)):
        first = wanted_ref[(me + step) & LAST] < n_slabs
        for i, block in enumerate(blocks):
            rows = pl.ds(i * EX_DEV, EX_DEV)
            out[0, rows, :] = block[2 * col_slabs + d]
            for k in range(col_slabs):
                out[1 + k, rows, :] = jnp.where(first, block[k], block[col_slabs + k])


def regroup(blocks, wanted, n_slabs):
    col_slabs = (blocks[0].shape[0] - len(SECOND)) // 2
    vmem = pl.BlockSpec(memory_space=pltpu.VMEM)
    part = jax.ShapeDtypeStruct((1 + col_slabs, len(blocks) * EX_DEV, LANES), jnp.float32)
    return pl.pallas_call(
        functools.partial(regroup_kernel, n_slabs),
        out_shape=[part] * len(SECOND),
        in_specs=[vmem] * (len(blocks) + 1),
        out_specs=[vmem] * len(SECOND),
        compiler_params=pltpu.CompilerParams(vmem_limit_bytes=SMALL_BYTES),
        name="regroup",
    )(*blocks, wanted)


def fisher_kernel(scale, n_parts, *refs):
    parts, vec_ref, (out_ref, vec_out, stack, full, sems) = refs[:n_parts], refs[n_parts], refs[-5:]
    store = pltpu.make_async_copy(vec_ref, vec_out, sems.at[0])
    store.start()
    examples, slabs = stack.shape[0], stack.shape[1] // LANES
    pieces = [part.at[i] for part in parts for i in range(part.shape[0])]
    rows = examples // len(pieces)
    for i, piece in enumerate(pieces):
        for k in range(slabs):
            stack[pl.ds(i * rows, rows), pl.ds(k * LANES, LANES)] = piece[k]
    own_rows, col_width = out_ref.shape[1:]
    start = 0
    if own_rows < LANES:
        start = (refs[n_parts + 1][lax.axis_index("dp")] * own_rows) % LANES
        start = pl.multiple_of(start, own_rows)
    row_high, row_low = split(stack[:, pl.ds(0, LANES)])
    row_wide = jnp.concatenate([row_high, row_high, row_low], axis=0)
    pieces = 2 if col_width % (2 * LANES) == 0 else 1
    size = col_width // pieces
    stores = [store]
    for c in range(pieces):
        col_high, col_low = split(stack[:, pl.ds(LANES + c * size, size)])
        col_wide = jnp.concatenate([col_high, col_low, col_high], axis=0)
        product = lax.dot_general(row_wide, col_wide, TN, preferred_element_type=jnp.float32)
        full[:, pl.ds(c * size, size)] = product * scale
        stores.append(
            pltpu.make_async_copy(
                full.at[pl.ds(start, own_rows), pl.ds(c * size, size)],
                out_ref.at[0, :, pl.ds(c * size, size)],
                sems.at[1 + c],
            )
        )
        stores[-1].start()
    for store in stores:
        store.wait()


def fisher(parts, vec, owner_map, own_rows):
    slabs = parts[0].shape[1]
    examples = sum(part.shape[0] * part.shape[2] for part in parts)
    col_width = (slabs - 1) * LANES
    hbm = pl.BlockSpec(memory_space=pl.ANY)
    owners = (owner_map,) if own_rows < LANES else ()
    return pl.pallas_call(
        functools.partial(fisher_kernel, 1.0 / examples, len(parts)),
        out_shape=(
            jax.ShapeDtypeStruct((1, own_rows, col_width), jnp.float32),
            jax.ShapeDtypeStruct(vec.shape, vec.dtype),
        ),
        in_specs=[pl.BlockSpec(memory_space=pltpu.VMEM)] * len(parts) + [hbm]
        + [pl.BlockSpec(memory_space=pltpu.SMEM)] * len(owners),
        out_specs=(hbm, hbm),
        scratch_shapes=[
            pltpu.VMEM((examples, slabs * LANES), jnp.float32),
            pltpu.VMEM((LANES, col_width), jnp.float32),
            pltpu.SemaphoreType.DMA((3,)),
        ],
        compiler_params=pltpu.CompilerParams(vmem_limit_bytes=SMALL_BYTES),
        name="fisher",
    )(*parts, vec, *owners)


def shards(
    o_inputs,
    o_gradients,
    up_inputs,
    up_gradients,
    o_in_proj,
    o_out_proj,
    up_in_proj,
    up_out_proj,
    segment_ids,
    owner_map,
):
    tensor_count = lax.axis_size("tensor")
    dp_count = lax.axis_size("dp")
    width = o_in_proj.shape[1] * o_out_proj.shape[1]
    col_width = width // tensor_count
    own_rows = 2 * width // dp_count
    (own,) = project(
        (o_inputs, o_gradients, up_inputs, up_gradients),
        (o_in_proj.T, o_out_proj.T, up_in_proj.T, up_out_proj.T),
    )
    wanted = jnp.broadcast_to((owner_map * own_rows // LANES)[:, None, None], (dp_count, EX_DEV, LANES))
    if tensor_count == 2:
        staged, wanted = stage(own, wanted)
        parts = (staged, lax.ppermute(own, "tensor", [(0, 1), (1, 0)]))
    else:
        parts = (lax.psum(own, "tensor"),)
    col_slabs = col_width // LANES
    if dp_count == len(FIRST) * len(SECOND) and own_rows == LANES:
        block = (2 * col_slabs + len(SECOND),)
        vec, *blocks = vectors(parts, segment_ids, wanted, col_width, [block] * len(FIRST))
        for n, step in enumerate(FIRST[1:], 1):
            blocks[n] = lax.ppermute(blocks[n], "dp", [(i, i ^ step) for i in range(dp_count)])
        recv = list(regroup(blocks, wanted, width // LANES))
        for n, step in enumerate(SECOND[1:], 1):
            recv[n] = lax.ppermute(recv[n], "dp", [(i, (i + step) & LAST) for i in range(dp_count)])
        recv = [part[None] for part in recv]
    else:
        vec, send = vectors(parts, segment_ids, wanted, col_width, [(dp_count, 1 + col_slabs)])
        recv = [lax.all_to_all(send, "dp", 0, 0, tiled=True)]
    fisher_block, example_vectors = fisher(recv, vec, owner_map, own_rows)
    return example_vectors, fisher_block


def solution(mesh):
    in_specs = (
        P("dp", "tensor"),
        P("dp", "tensor"),
        P("dp", "tensor"),
        P("dp", "tensor"),
        P("tensor", None),
        P("tensor", None),
        P("tensor", None),
        P("tensor", None),
        P("dp", None),
        P(),
    )
    out_specs = (P(None, "dp", "tensor"), P("dp", None, "tensor"))
    return jax.shard_map(shards, mesh=mesh, in_specs=in_specs, out_specs=out_specs, check_vma=False)
```

```python
import functools

import jax
import jax.numpy as jnp
from jax import lax
from jax.experimental import pallas as pl
from jax.experimental.pallas import tpu as pltpu
from jax.sharding import PartitionSpec as P

TOK_DEV = 256
EX_DEV = 4
LANES = 128
NT = (((1,), (1,)), ((), ()))
TN = (((0,), (0,)), ((), ()))
PIECE = 4096
FIRST = (0, 3, 2, 1)
SECOND = (0, 4, 8, 12)
LAST = len(FIRST) * len(SECOND) - 1
VMEM_BYTES = 54976 * 2**10
SMALL_BYTES = 8 * 2**20


def chunk_plan(widths):
    plan = []
    for which in sorted(range(len(widths)), key=lambda i: -widths[i]):
        start = 0
        while start < widths[which]:
            size = (widths[which] - start) % PIECE or PIECE
            plan.append((which, start, size))
            start += size
    return plan


def split(x):
    high = x.astype(jnp.bfloat16)
    return high, (x - high.astype(jnp.float32)).astype(jnp.bfloat16)


def project_kernel(plan, halves, *refs):
    x_hbm, w_hbm, outs = refs[0:4], refs[4:8], refs[8:9]
    x_vmem, w_vmem, x_sem, w_sem = refs[9:13], refs[13:17], refs[17], refs[18]
    w_copies, x_copies = [], []
    for n, (i, start, size) in enumerate(plan):
        piece = (slice(None), pl.ds(start, size))
        w_copies.append(pltpu.make_async_copy(w_hbm[i].at[piece], w_vmem[i].at[piece], w_sem.at[n]))
        x_copies.append(pltpu.make_async_copy(x_hbm[i].at[piece], x_vmem[i].at[piece], x_sem.at[n]))
        x_copies[n].start()
        w_copies[n].start()
    tokens, rank = x_vmem[0].shape[0], w_vmem[0].shape[0]
    part = tokens // halves
    totals = {}
    for n, (i, start, size) in enumerate(plan):
        w_copies[n].wait()
        x_copies[n].wait()
        w = w_vmem[i][:, pl.ds(start, size)]
        for h in range(halves):
            x = x_vmem[i][pl.ds(h * part, part), pl.ds(start, size)]
            product = lax.dot_general(x, w, NT, preferred_element_type=jnp.float32)
            totals[i, h] = product if start == 0 else totals[i, h] + product
    for i in range(4):
        for h in range(halves):
            low = totals[i, h].T
            for out in outs:
                out[h, pl.ds(i * rank, rank), :] = low


def project(xs, ws):
    plan = chunk_plan([x.shape[1] for x in xs])
    tokens, rank = xs[0].shape[0], ws[0].shape[0]
    halves = tokens // LANES
    low = jax.ShapeDtypeStruct((halves, 4 * rank, LANES), jnp.float32)
    return pl.pallas_call(
        functools.partial(project_kernel, plan, halves),
        out_shape=(low,),
        in_specs=[pl.BlockSpec(memory_space=pl.ANY)] * 8,
        out_specs=(pl.BlockSpec(memory_space=pltpu.VMEM),),
        scratch_shapes=[pltpu.VMEM(x.shape, x.dtype) for x in xs]
        + [pltpu.VMEM(w.shape, w.dtype) for w in ws]
        + [pltpu.SemaphoreType.DMA((len(plan),))] * 2,
        compiler_params=pltpu.CompilerParams(vmem_limit_bytes=VMEM_BYTES),
        name="project",
    )(*xs, *ws)


def stage_kernel(low_ref, wanted_ref, low_out, wanted_out):
    low_out[...] = low_ref[...]
    wanted_out[...] = wanted_ref[...]


def stage(low, wanted):
    vmem = pl.BlockSpec(memory_space=pltpu.VMEM)
    return pl.pallas_call(
        stage_kernel,
        out_shape=[jax.ShapeDtypeStruct(x.shape, x.dtype) for x in (low, wanted)],
        in_specs=[vmem] * 2,
        out_specs=[vmem] * 2,
        compiler_params=pltpu.CompilerParams(vmem_limit_bytes=SMALL_BYTES),
        name="stage",
    )(low, wanted)


def vectors_kernel(n_parts, n_sends, *refs):
    parts, seg_ref, wanted_ref, vec_ref = refs[:n_parts], *refs[n_parts : n_parts + 3]
    send_refs, slabs = refs[n_parts + 3 : n_parts + 3 + n_sends], refs[n_parts + 3 + n_sends]
    halves, rank = parts[0].shape[0], parts[0].shape[1] // 4
    fold = LANES // rank
    n_slabs = rank // fold
    col_slabs = vec_ref.shape[2] // LANES
    seg = seg_ref[...]
    lane = lax.broadcasted_iota(jnp.int32, (EX_DEV * n_slabs, LANES), 1)
    scale = (EX_DEV / TOK_DEV) ** 0.5

    def total(index):
        sums = [functools.reduce(lambda a, b: a + b, [part[h, index, :] for part in parts]) for h in range(halves)]
        return jnp.concatenate(sums, axis=1)

    for p in range(2):
        in_high, in_low = split(total(pl.ds(2 * p * rank, rank)))
        in_wide = jnp.concatenate([in_high, in_low, in_high], axis=1)
        in_wide = jnp.concatenate([in_wide] * fold, axis=0)
        rows = []
        for b in range(fold):
            out_rows = total(pl.ds((2 * p + 1) * rank + b, n_slabs, stride=fold))
            rows += [jnp.where(seg == e, out_rows, 0.0) for e in range(EX_DEV)]
        out_high, out_low = split(jnp.concatenate(rows, axis=0))
        out_wide = jnp.concatenate([out_high, out_high, out_low], axis=1)
        outer = lax.dot_general(out_wide, in_wide, NT, preferred_element_type=jnp.float32)
        flat = outer[: EX_DEV * n_slabs]
        for b in range(1, fold):
            block = outer[b * EX_DEV * n_slabs : (b + 1) * EX_DEV * n_slabs]
            flat = jnp.where(lane // rank == b, block, flat)
        flat = flat * scale
        for g in range(n_slabs):
            slabs[p * n_slabs + g] = jnp.concatenate(
                [flat[e * n_slabs + g : e * n_slabs + g + 1] for e in range(EX_DEV)], axis=0
            )
    t = lax.axis_index("tensor")
    columns = [[slabs[p * n_slabs + t * col_slabs + k] for k in range(col_slabs)] for p in range(2)]
    for p in range(2):
        for k in range(col_slabs):
            vec_ref[p, :, pl.ds(k * LANES, LANES)] = columns[p][k]
    rows = [slabs[s] for s in range(2 * n_slabs)]
    for j in range(wanted_ref.shape[0]):
        wanted = wanted_ref[j]
        row_slab = rows[0]
        for s in range(1, 2 * n_slabs):
            row_slab = jnp.where(wanted == s, rows[s], row_slab)
        if n_sends > 1:
            refs[-1][j] = row_slab
            continue
        send_refs[0][j, 0] = row_slab
        for k in range(col_slabs):
            send_refs[0][j, 1 + k] = jnp.where(wanted < n_slabs, columns[0][k], columns[1][k])
    if n_sends > 1:
        me = lax.axis_index("dp")
        for target, send_ref in zip(FIRST, send_refs):
            for p in range(2):
                for k in range(col_slabs):
                    send_ref[p * col_slabs + k] = columns[p][k]
            for d, step in enumerate(SECOND):
                send_ref[2 * col_slabs + d] = refs[-1][((me ^ target) + step) & LAST]


def vectors(parts, segments, wanted, col_width, sends):
    n_slabs = (parts[0].shape[1] // 4) ** 2 // LANES
    vmem = pl.BlockSpec(memory_space=pltpu.VMEM)
    return pl.pallas_call(
        functools.partial(vectors_kernel, len(parts), len(sends)),
        out_shape=[jax.ShapeDtypeStruct((2, EX_DEV, col_width), jnp.float32)]
        + [jax.ShapeDtypeStruct(shape + (EX_DEV, LANES), jnp.float32) for shape in sends],
        in_specs=[vmem] * (len(parts) + 2),
        out_specs=[vmem] * (1 + len(sends)),
        scratch_shapes=[
            pltpu.VMEM((2 * n_slabs, EX_DEV, LANES), jnp.float32),
            pltpu.VMEM((wanted.shape[0], EX_DEV, LANES), jnp.float32),
        ],
        compiler_params=pltpu.CompilerParams(vmem_limit_bytes=SMALL_BYTES),
        name="vectors",
    )(*parts, segments, wanted)


def regroup_kernel(n_slabs, *refs):
    blocks, wanted_ref, outs = refs[: len(FIRST)], refs[len(FIRST)], refs[len(FIRST) + 1 :]
    col_slabs = (blocks[0].shape[0] - len(SECOND)) // 2
    me = lax.axis_index("dp")
    for d, (step, out) in enumerate(zip(SECOND, outs)):
        first = wanted_ref[(me + step) & LAST] < n_slabs
        for i, block in enumerate(blocks):
            rows = pl.ds(i * EX_DEV, EX_DEV)
            out[0, rows, :] = block[2 * col_slabs + d]
            for k in range(col_slabs):
                out[1 + k, rows, :] = jnp.where(first, block[k], block[col_slabs + k])


def regroup(blocks, wanted, n_slabs):
    col_slabs = (blocks[0].shape[0] - len(SECOND)) // 2
    vmem = pl.BlockSpec(memory_space=pltpu.VMEM)
    part = jax.ShapeDtypeStruct((1 + col_slabs, len(blocks) * EX_DEV, LANES), jnp.float32)
    return pl.pallas_call(
        functools.partial(regroup_kernel, n_slabs),
        out_shape=[part] * len(SECOND),
        in_specs=[vmem] * (len(blocks) + 1),
        out_specs=[vmem] * len(SECOND),
        compiler_params=pltpu.CompilerParams(vmem_limit_bytes=SMALL_BYTES),
        name="regroup",
    )(*blocks, wanted)


def fisher_kernel(scale, n_parts, *refs):
    parts, vec_ref, (out_ref, vec_out, stack, full, sems) = refs[:n_parts], refs[n_parts], refs[-5:]
    store = pltpu.make_async_copy(vec_ref, vec_out, sems.at[0])
    examples, slabs = stack.shape[0], stack.shape[1] // LANES
    pieces = [part.at[i] for part in parts for i in range(part.shape[0])]
    rows = examples // len(pieces)
    for i, piece in enumerate(pieces):
        for k in range(slabs):
            stack[pl.ds(i * rows, rows), pl.ds(k * LANES, LANES)] = piece[k]
    store.start()
    own_rows, col_width = out_ref.shape[1:]
    start = 0
    if own_rows < LANES:
        start = (refs[n_parts + 1][lax.axis_index("dp")] * own_rows) % LANES
        start = pl.multiple_of(start, own_rows)
    row_high, row_low = split(stack[:, pl.ds(0, LANES)])
    row_wide = jnp.concatenate([row_high, row_high, row_low], axis=0)
    pieces = 2 if col_width % (2 * LANES) == 0 else 1
    size = col_width // pieces
    stores = [store]
    for c in range(pieces):
        col_high, col_low = split(stack[:, pl.ds(LANES + c * size, size)])
        col_wide = jnp.concatenate([col_high, col_low, col_high], axis=0)
        product = lax.dot_general(row_wide, col_wide, TN, preferred_element_type=jnp.float32)
        full[:, pl.ds(c * size, size)] = product * scale
        stores.append(
            pltpu.make_async_copy(
                full.at[pl.ds(start, own_rows), pl.ds(c * size, size)],
                out_ref.at[0, :, pl.ds(c * size, size)],
                sems.at[1 + c],
            )
        )
        stores[-1].start()
    for store in stores:
        store.wait()


def fisher(parts, vec, owner_map, own_rows):
    slabs = parts[0].shape[1]
    examples = sum(part.shape[0] * part.shape[2] for part in parts)
    col_width = (slabs - 1) * LANES
    hbm = pl.BlockSpec(memory_space=pl.ANY)
    owners = (owner_map,) if own_rows < LANES else ()
    return pl.pallas_call(
        functools.partial(fisher_kernel, 1.0 / examples, len(parts)),
        out_shape=(
            jax.ShapeDtypeStruct((1, own_rows, col_width), jnp.float32),
            jax.ShapeDtypeStruct(vec.shape, vec.dtype),
        ),
        in_specs=[pl.BlockSpec(memory_space=pltpu.VMEM)] * len(parts) + [hbm]
        + [pl.BlockSpec(memory_space=pltpu.SMEM)] * len(owners),
        out_specs=(hbm, hbm),
        scratch_shapes=[
            pltpu.VMEM((examples, slabs * LANES), jnp.float32),
            pltpu.VMEM((LANES, col_width), jnp.float32),
            pltpu.SemaphoreType.DMA((3,)),
        ],
        compiler_params=pltpu.CompilerParams(vmem_limit_bytes=SMALL_BYTES),
        name="fisher",
    )(*parts, vec, *owners)


def shards(
    o_inputs,
    o_gradients,
    up_inputs,
    up_gradients,
    o_in_proj,
    o_out_proj,
    up_in_proj,
    up_out_proj,
    segment_ids,
    owner_map,
):
    tensor_count = lax.axis_size("tensor")
    dp_count = lax.axis_size("dp")
    width = o_in_proj.shape[1] * o_out_proj.shape[1]
    col_width = width // tensor_count
    own_rows = 2 * width // dp_count
    (own,) = project(
        (o_inputs, o_gradients, up_inputs, up_gradients),
        (o_in_proj.T, o_out_proj.T, up_in_proj.T, up_out_proj.T),
    )
    wanted = jnp.broadcast_to((owner_map * own_rows // LANES)[:, None, None], (dp_count, EX_DEV, LANES))
    if tensor_count == 2:
        staged, wanted = stage(own, wanted)
        parts = (staged, lax.ppermute(own, "tensor", [(0, 1), (1, 0)]))
    else:
        parts = (lax.psum(own, "tensor"),)
    col_slabs = col_width // LANES
    if dp_count == len(FIRST) * len(SECOND) and own_rows == LANES:
        block = (2 * col_slabs + len(SECOND),)
        vec, *blocks = vectors(parts, segment_ids, wanted, col_width, [block] * len(FIRST))
        for n, step in enumerate(FIRST[1:], 1):
            blocks[n] = lax.ppermute(blocks[n], "dp", [(i, i ^ step) for i in range(dp_count)])
        recv = list(regroup(blocks, wanted, width // LANES))
        for n, step in enumerate(SECOND[1:], 1):
            recv[n] = lax.ppermute(recv[n], "dp", [(i, (i + step) & LAST) for i in range(dp_count)])
        recv = [part[None] for part in recv]
    else:
        vec, send = vectors(parts, segment_ids, wanted, col_width, [(dp_count, 1 + col_slabs)])
        recv = [lax.all_to_all(send, "dp", 0, 0, tiled=True)]
    fisher_block, example_vectors = fisher(recv, vec, owner_map, own_rows)
    return example_vectors, fisher_block


def solution(mesh):
    in_specs = (
        P("dp", "tensor"),
        P("dp", "tensor"),
        P("dp", "tensor"),
        P("dp", "tensor"),
        P("tensor", None),
        P("tensor", None),
        P("tensor", None),
        P("tensor", None),
        P("dp", None),
        P(),
    )
    out_specs = (P(None, "dp", "tensor"), P("dp", None, "tensor"))
    return jax.shard_map(shards, mesh=mesh, in_specs=in_specs, out_specs=out_specs, check_vma=False)
```
